256 devices in a mesh: blk: 8 (over y, x_hi), rep: 32 (over x_lo, z, core).
Axes of the slice: x: 4 (x_hi: 2, x_lo: 2; x = x_hi * 2 + x_lo), y: 4, z: 8, core: 2. Of those that a mesh axis runs over, the one named last changes fastest.
Arguments:
- node_feats: bfloat16 [98304, 128], P(('blk', 'rep')), may hold values from -6 to 6
- block_vals: bfloat16 [8, 32, 8, 40, 128, 128], P('blk', 'rep'), may hold values from 0.00049972534 to 0.049804688
- block_rows: int32 [8, 32, 8, 40], P('blk', 'rep'), may hold values from 0 to 95
- block_cols: int32 [8, 32, 8, 40], P('blk', 'rep'), may hold values from 0 to 2
- block_count: int32 [8, 32, 8], P('blk', 'rep'), may hold values from 1 to 40, as said below
- weight: bfloat16 [128, 256], replicated, may hold values from -0.5 to 0.5
Outputs:
- layer_out: bfloat16 [98304, 256], P(('blk', 'rep'))
The draws below stay inside these ranges and needn't reach their ends.
Inputs may be any that keep to these rules, and one draw needn't show every extreme that they name: Only the first block_count[b, r, j] slots of list (b, r, j) are live; the values, rows and columns of later slots are ignored. The largest count 40 is reached in every draw.
All inputs are finite; a program needn't handle non-finite values.
Results may differ from the reference program's by a relative error of at most 0.0011.
Values may be sent and summed in bfloat16 or wider, within the bound.
No kernel may reach another device: no remote copies, remote signals or barrier semaphores. Data moves between devices by JAX's collectives and lax.ppermute only.
A program may use at most 128 MiB of HBM per device.

```python
import math
import jax
import jax.numpy as jnp
import numpy as np
from jax import lax

F = 128
H = 256
BS = 128
SLOTS = 40
PIECE_BLK = 3
PANEL_BLK = 96
NODES = 98304
N_BLK = 8
N_REP = 32


def draw_block_count(key, part):
    dims_all = (N_BLK, N_REP, N_BLK)
    total = N_BLK * N_REP * N_BLK
    key_light, key_hubs, key_heavy, key_spot = jax.random.split(key, 4)
    light_load = jax.random.randint(key_light, dims_all, max(1, SLOTS // 8), SLOTS // 3 + 1)
    hub_lists = jax.random.randint(key_hubs, dims_all, 0, 8) == 0
    heavy_load = SLOTS - jax.random.randint(key_heavy, dims_all, 0, max(1, SLOTS // 8))
    counts = jnp.where(hub_lists, heavy_load, light_load)
    hotspot = jax.random.randint(key_spot, (), 0, total)
    flattened = jnp.where(jnp.arange(total) == hotspot, SLOTS, counts.reshape(-1))
    return flattened.reshape(dims_all).astype(jnp.int32)


def with_ends(entries, own_key, smallest, largest):
    shape = entries.shape
    index_at = [jax.random.randint(jax.random.fold_in(own_key, axis), (), 0, shape[axis]) for axis in range(len(shape))]
    entries = entries.at[tuple(index_at)].set(smallest)
    longest = shape.index(max(shape))
    index_at[longest] = (index_at[longest] + 1) % shape[longest]
    return entries.at[tuple(index_at)].set(largest)


def levels(stream_key, dims, shards, low, high):
    gain = 1.0
    for dim, blocks in shards:
        heights = jax.random.uniform(jax.random.fold_in(jax.random.fold_in(stream_key, 6), dim), (blocks,), jnp.float32, low / len(shards), high / len(shards))
        gain = gain * jnp.repeat(jnp.exp(heights), dims[dim] // blocks).reshape((-1,) + (1,) * (len(dims) - 1 - dim))
    return gain


def rank_bounds(amount, skew):
    portions = [(1 << 20) // math.isqrt(rank ** skew) + 1 for rank in range(1, amount + 1)]
    deviation = 1 + sum(portions) // (1 << 30)
    return np.cumsum(np.array([max(1, weight // deviation) for weight in portions]))


def ranked_ids(key, dims, count, slope):
    table = rank_bounds(count, slope)
    lot = jax.random.randint(jax.random.fold_in(key, 1), dims, 0, int(table[count - 1]))
    grade = jnp.searchsorted(jnp.asarray(table, jnp.int32), lot, side="right")
    return jax.random.permutation(jax.random.fold_in(key, 2), count)[grade].astype(jnp.int32)


def noise(stream_key, extent, width, reach, shards=(), kind=jnp.bfloat16):
    drawn = width * jax.random.normal(stream_key, extent, jnp.float32)
    if shards:
        drawn = drawn * levels(stream_key, extent, shards, -0.22, 0.18)
    return jnp.clip(drawn, -reach, reach).astype(kind)


def setup_inputs(seed: int = 0) -> dict:
    arg_keys = jax.random.split(jax.random.key(seed), 7)
    return {
        "node_feats": noise(arg_keys[0], (NODES, F), 1.0, 6.0, ((0, 256),)),
        "block_vals": jnp.clip(jnp.exp(math.log(0.049804688) - 4.6018058 * jax.random.uniform(arg_keys[1], (N_BLK, N_REP, N_BLK, SLOTS, BS, BS), jnp.float32) ** levels(arg_keys[1], (N_BLK, N_REP, N_BLK, SLOTS, BS, BS), ((0, 8), (1, 32)), -0.2, 0.2)), 0.00049972534, 0.049804688).astype(jnp.bfloat16),
        "block_rows": with_ends(ranked_ids(arg_keys[2], (N_BLK, N_REP, N_BLK, SLOTS), PANEL_BLK, 2), jax.random.fold_in(arg_keys[2], 3), 0, PANEL_BLK - 1).astype(jnp.int32),
        "block_cols": with_ends(jax.random.randint(arg_keys[3], (N_BLK, N_REP, N_BLK, SLOTS), 0, PIECE_BLK), jax.random.fold_in(arg_keys[3], 1), 0, PIECE_BLK - 1).astype(jnp.int32),
        "block_count": draw_block_count(jax.random.fold_in(arg_keys[6], 71), 0),
        "weight": noise(arg_keys[5], (F, H), F ** -0.5, 0.5),
    }


def reference(node_feats, block_vals, block_rows, block_cols, block_count, weight):
    pieces = node_feats.reshape(N_BLK, N_REP, PIECE_BLK, BS, F).astype(jnp.float32)
    source = jnp.arange(N_BLK, dtype=jnp.int32)[None, :, None]
    replica = jnp.arange(N_REP, dtype=jnp.int32)[:, None, None]
    slot_ids = jnp.arange(SLOTS, dtype=jnp.int32)

    def one_panel(inputs):
        vals_panel, rows_panel, cols_panel, count_panel = inputs
        gathered = pieces[source, replica, cols_panel]
        products = jnp.einsum("rjsab,rjsbf->rjsaf", vals_panel.astype(jnp.float32), gathered)
        in_use = slot_ids[None, None, :] < count_panel[:, :, None]
        products = jnp.where(in_use[:, :, :, None, None], products, jnp.float32(0.0))
        panel_sum = jnp.zeros((PANEL_BLK, BS, F), jnp.float32)
        panel_sum = panel_sum.at[rows_panel.reshape(-1)].add(products.reshape(-1, BS, F))
        return panel_sum

    panels = lax.map(one_panel, (block_vals, block_rows, block_cols, block_count))
    agg = panels.reshape(NODES, F)
    result = jnp.dot(agg, weight.astype(jnp.float32), precision=lax.Precision.HIGHEST)
    return jnp.maximum(result, 0.0).astype(jnp.bfloat16)
```

```python
import functools

import jax
import jax.numpy as jnp
from jax import lax
from jax.experimental import pallas as pl
from jax.experimental.pallas import tpu as pltpu
from jax.sharding import PartitionSpec as P

BS = 128
F = 128
H = 256
SLOTS = 40
LISTS = 8
PIECE_BLK = 3
PIECE_ROWS = PIECE_BLK * BS
PANEL_BLK = 96
GROUP = 8
GROUPS = SLOTS // GROUP
MSG = PIECE_ROWS + 16
MIB = 1 << 20


def params(mib):
    return pltpu.CompilerParams(vmem_limit_bytes=mib * MIB)


def quantize(block):
    peak = jnp.maximum(jnp.max(jnp.abs(block), axis=0, keepdims=True), 1e-32)
    exponent = jnp.ceil(jnp.log2(peak) + 0.001)
    scaled = block * (jnp.exp2(-exponent) * 32766.0)
    return jnp.round(scaled).astype(jnp.int32).astype(jnp.int16), exponent


def step_size(exponent):
    return jnp.exp2(exponent) * (1.0 / 32766.0)


def write_message(out_ref, index, blocks):
    row = lax.broadcasted_iota(jnp.int32, (16, F), 0)
    tail = jnp.zeros((16, F), jnp.float32)
    for i, block in enumerate(blocks):
        whole, exponent = quantize(block)
        out_ref[index, i * BS : (i + 1) * BS, :] = whole
        tail = jnp.where(row == i, exponent, tail)
    out_ref[index, PIECE_ROWS:MSG, :] = tail.astype(jnp.int32).astype(jnp.int16)


def read_message(ref, index):
    tail = ref[index, PIECE_ROWS:MSG, :].astype(jnp.int32).astype(jnp.float32)
    size = step_size(tail)
    blocks = []
    for i in range(PIECE_BLK):
        whole = ref[index, i * BS : (i + 1) * BS, :].astype(jnp.int32).astype(jnp.float32)
        blocks.append(whole * size[i : i + 1, :])
    return blocks


def add(first, second):
    return [a + b for a, b in zip(first, second)]


def read_own(ref, index):
    return [ref[index, i * BS : (i + 1) * BS, :] for i in range(PIECE_BLK)]


def product_kernel(
    place_ref, count_ref, rows_ref, cols_ref,
    x0_ref, x1_ref, xm_ref, xp_ref, c0_ref, c1_ref, vals_ref,
    own_ref, msg_ref,
    panel, pieces, vals, x_sems, vals_sems, own_sem,
):
    y, x_hi, core = place_ref[0], place_ref[1], place_ref[2]

    def piece(shift, flip):
        return lax.rem(y + shift, 4) * 2 + jnp.where(flip, 1 - x_hi, x_hi)

    copies = [
        pltpu.make_async_copy(source, pieces.at[index], x_sems.at[k])
        for k, (source, index) in enumerate([
            (x0_ref, piece(0, False)),
            (x1_ref, piece(0, True)),
            (xm_ref.at[0], piece(3, False)),
            (xm_ref.at[1], piece(3, True)),
            (xp_ref.at[0], piece(1, False)),
            (xp_ref.at[1], piece(1, True)),
            (c0_ref, piece(2, False)),
            (c1_ref, piece(2, True)),
        ])
    ]
    for copy in copies:
        copy.start()

    def group_copy(j, g):
        base = pl.multiple_of(j * SLOTS + g * GROUP, GROUP)
        return pltpu.make_async_copy(
            vals_ref.at[pl.ds(base, GROUP)], vals.at[pl.ds(base, GROUP)], vals_sems.at[j * GROUPS + g]
        )

    def groups_of(j):
        return lax.div(jnp.clip(count_ref[j], 0, SLOTS) + (GROUP - 1), GROUP)

    @pl.loop(0, LISTS)
    def _(j):
        @pl.loop(0, groups_of(j))
        def _(g):
            group_copy(j, g).start()

    @pl.loop(0, PANEL_BLK)
    def _(k):
        panel[k] = jnp.zeros((BS, F), jnp.float32)

    for copy in copies:
        copy.wait()

    @pl.loop(0, LISTS)
    def _(j):
        count = count_ref[j]

        @pl.loop(0, groups_of(j))
        def _(g):
            group_copy(j, g).wait()
            for half in range(2):
                products, rows = [], []
                for u in range(half * GROUP // 2, (half + 1) * GROUP // 2):
                    q = g * GROUP + u
                    slot = j * SLOTS + q
                    live = q < count
                    rows.append(jnp.where(live, rows_ref[slot], PANEL_BLK))
                    col = jnp.where(live, cols_ref[slot], 0)
                    products.append(
                        jnp.dot(
                            vals[slot],
                            pieces[j, pl.ds(pl.multiple_of(col * BS, BS), BS), :],
                            preferred_element_type=jnp.float32,
                        )
                    )
                for row, product in zip(rows, products):
                    panel[row] += product

    def own_copy(p):
        base = (2 * p + core) * PIECE_BLK
        return [
            pltpu.make_async_copy(
                panel.at[base + i], own_ref.at[p, pl.ds(i * BS, BS)], own_sem.at[p * PIECE_BLK + i]
            )
            for i in range(PIECE_BLK)
        ]

    @pl.loop(0, 16)
    def _(p):
        for copy in own_copy(p):
            copy.start()

    @pl.loop(0, 16)
    def _(p):
        base = (2 * p + 1 - core) * PIECE_BLK
        write_message(msg_ref, p, [panel[base + i] for i in range(PIECE_BLK)])

    @pl.loop(0, 16)
    def _(p):
        for copy in own_copy(p):
            copy.wait()


def products(place, counts, rows, cols, pieces, vals):
    return pl.pallas_call(
        product_kernel,
        out_shape=(
            jax.ShapeDtypeStruct((16, PIECE_ROWS, F), jnp.float32),
            jax.ShapeDtypeStruct((16, MSG, F), jnp.int16),
        ),
        in_specs=[pl.BlockSpec(memory_space=pltpu.SMEM)] * 4 + [pl.BlockSpec(memory_space=pl.ANY)] * 7,
        out_specs=(pl.BlockSpec(memory_space=pl.ANY), pl.BlockSpec(memory_space=pltpu.VMEM)),
        scratch_shapes=[
            pltpu.VMEM((PANEL_BLK + 1, BS, F), jnp.float32),
            pltpu.VMEM((LISTS, PIECE_ROWS, F), jnp.bfloat16),
            pltpu.VMEM((LISTS * SLOTS, BS, BS), jnp.bfloat16),
            pltpu.SemaphoreType.DMA((8,)),
            pltpu.SemaphoreType.DMA((LISTS * GROUPS,)),
            pltpu.SemaphoreType.DMA((16 * PIECE_BLK,)),
        ],
        compiler_params=params(40),
        name="block_products",
    )(place, counts, rows, cols, *pieces, vals)


def x_kernel(place_ref, own_ref, rc_ref, out_ref):
    other = 1 - place_ref[3]

    @pl.loop(0, 8)
    def _(z):
        p = other * 8 + z
        write_message(out_ref, z, add(read_own(own_ref, p), read_message(rc_ref, p)))


def z_kernel(place_ref, own_ref, rc_ref, rx_ref, out_ref):
    x_lo, z = place_ref[3], place_ref[4]

    @pl.loop(0, 7)
    def _(s):
        target = lax.rem(z + s + 1, 8)
        p = x_lo * 8 + target
        total = add(add(read_own(own_ref, p), read_message(rc_ref, p)), read_message(rx_ref, target))
        write_message(out_ref, s, total)


def stage(kernel, name, place, arrays, count):
    return pl.pallas_call(
        kernel,
        out_shape=jax.ShapeDtypeStruct((count, MSG, F), jnp.int16),
        in_specs=[pl.BlockSpec(memory_space=pltpu.SMEM)] + [pl.BlockSpec(memory_space=pltpu.VMEM)] * len(arrays),
        out_specs=pl.BlockSpec(memory_space=pltpu.VMEM),
        compiler_params=params(24),
        name=name,
    )(place, *arrays)


def last_kernel(place_ref, own_ref, rc_ref, rx_ref, *refs):
    weight_ref, out_ref = refs[7], refs[8]
    x_lo, z = place_ref[3], place_ref[4]
    p = x_lo * 8 + z
    total = add(add(read_own(own_ref, p), read_message(rc_ref, p)), read_message(rx_ref, z))
    for ref in refs[:7]:
        total = add(total, read_message(ref, 0))
    weight = weight_ref[...]
    for i, block in enumerate(total):
        high = block.astype(jnp.bfloat16)
        rest = block - high.astype(jnp.float32)
        middle = rest.astype(jnp.bfloat16)
        low = (rest - middle.astype(jnp.float32)).astype(jnp.bfloat16)
        result = jnp.dot(low, weight, preferred_element_type=jnp.float32)
        result += jnp.dot(middle, weight, preferred_element_type=jnp.float32)
        result += jnp.dot(high, weight, preferred_element_type=jnp.float32)
        out_ref[i * BS : (i + 1) * BS, :] = jnp.maximum(result, 0.0).astype(jnp.bfloat16)


def last(place, own, rc, rx, rz, weight):
    return pl.pallas_call(
        last_kernel,
        out_shape=jax.ShapeDtypeStruct((PIECE_ROWS, H), jnp.bfloat16),
        in_specs=[pl.BlockSpec(memory_space=pltpu.SMEM)] + [pl.BlockSpec(memory_space=pltpu.VMEM)] * 11,
        out_specs=pl.BlockSpec(memory_space=pltpu.VMEM),
        compiler_params=params(24),
        name="layer",
    )(place, own, rc, rx, *rz, weight)


def blk_pairs(dy, flip):
    return [(y * 2 + h, ((y + dy) % 4) * 2 + (h ^ flip)) for y in range(4) for h in range(2)]


def rep_pairs(dx, dz, dc):
    return [
        (x * 16 + z * 2 + c, (x ^ dx) * 16 + ((z + dz) % 8) * 2 + (c ^ dc))
        for x in range(2) for z in range(8) for c in range(2)
    ]


def gather_pieces(own):
    flipped = lax.ppermute(own, "blk", blk_pairs(0, 1))
    both = jnp.stack([own, flipped])
    below = lax.ppermute(both, "blk", blk_pairs(1, 0))
    above = lax.ppermute(both, "blk", blk_pairs(3, 0))
    far_own = lax.ppermute(below[0], "blk", blk_pairs(1, 0))
    far_flipped = lax.ppermute(above[1], "blk", blk_pairs(3, 0))
    return own, flipped, below, above, far_own, far_flipped


def local(node_feats, block_vals, block_rows, block_cols, block_count, weight):
    blk = lax.axis_index("blk")
    rep = lax.axis_index("rep")
    place = jnp.stack([blk // 2, blk % 2, rep % 2, rep // 16, (rep // 2) % 8]).astype(jnp.int32)
    pieces = gather_pieces(node_feats)
    own, message = products(
        place, block_count.reshape(-1), block_rows.reshape(-1), block_cols.reshape(-1),
        pieces, block_vals.reshape(LISTS * SLOTS, BS, BS),
    )
    rc = lax.ppermute(message, "rep", rep_pairs(0, 0, 1))
    rx = lax.ppermute(stage(x_kernel, "across_x", place, (own, rc), 8), "rep", rep_pairs(1, 0, 0))
    to_z = stage(z_kernel, "across_z", place, (own, rc, rx), 7)
    rz = [lax.ppermute(to_z[s : s + 1], "rep", rep_pairs(0, s + 1, 0)) for s in range(7)]
    return last(place, own, rc, rx, rz, weight)


def solution(mesh):
    return jax.shard_map(
        local,
        mesh=mesh,
        in_specs=(
            P(("blk", "rep"), None),
            P("blk", "rep", None, None, None, None),
            P("blk", "rep", None, None),
            P("blk", "rep", None, None),
            P("blk", "rep", None),
            P(),
        ),
        out_specs=P(("blk", "rep"), None),
        check_vma=False,
    )
```

```python
import functools

import jax
import jax.numpy as jnp
from jax import lax
from jax.experimental import pallas as pl
from jax.experimental.pallas import tpu as pltpu
from jax.sharding import PartitionSpec as P

BS = 128
F = 128
H = 256
SLOTS = 40
LISTS = 8
PIECE_BLK = 3
PIECE_ROWS = PIECE_BLK * BS
HALF = PIECE_ROWS // 2
PANEL_BLK = 96
GROUP = 8
GROUPS = SLOTS // GROUP
TOP = 32766.0
MIB = 1 << 20

FIRST, SECOND = (0, 2), (2, 1)


def message_rows(blocks):
    return blocks * BS + 16


SMEM = pl.BlockSpec(memory_space=pltpu.SMEM)
VMEM = pl.BlockSpec(memory_space=pltpu.VMEM)
ANY = pl.BlockSpec(memory_space=pl.ANY)


def call(kernel, name, out_shape, in_specs, out_specs, args, us, mib=24, **more):
    return pl.pallas_call(
        kernel,
        out_shape=out_shape,
        in_specs=in_specs,
        out_specs=out_specs,
        compiler_params=pltpu.CompilerParams(vmem_limit_bytes=mib * MIB),
        cost_estimate=pl.CostEstimate(flops=0, bytes_accessed=int(us * 3.0e6), transcendentals=0),
        name=name,
        **more,
    )(*args)


def groups_of(count):
    return lax.div(jnp.clip(count, 0, SLOTS) + (GROUP - 1), GROUP)


def add_list(panel, piece, vals, count_ref, rows_ref, cols_ref, j, before=None):
    count = count_ref[0, j]

    @pl.loop(0, groups_of(count))
    def _(g):
        if before is not None:
            before(g)
        for half in range(2):
            products, rows = [], []
            for u in range(half * GROUP // 2, (half + 1) * GROUP // 2):
                q = g * GROUP + u
                live = q < count
                rows.append(jnp.where(live, rows_ref[j, q], PANEL_BLK))
                col = jnp.where(live, cols_ref[j, q], 0)
                products.append(
                    jnp.dot(
                        vals[j * SLOTS + q],
                        piece[pl.ds(pl.multiple_of(col * BS, BS), BS), :],
                        preferred_element_type=jnp.float32,
                    )
                )
            for row, product in zip(rows, products):
                panel[row] += product


def piece_of(place_ref, shift, flip):
    x_hi = place_ref[1]
    return lax.rem(place_ref[0] + shift, 4) * 2 + (1 - x_hi if flip else x_hi)


def first_products(place_ref, count_ref, rows_ref, cols_ref, own_ref, vals_ref, panel, vals, sems):
    def copy(j, g):
        base = pl.multiple_of(j * SLOTS + g * GROUP, GROUP)
        return pltpu.make_async_copy(
            vals_ref.at[pl.ds(base, GROUP)], vals.at[pl.ds(base, GROUP)], sems.at[j * GROUPS + g]
        )

    mine = piece_of(place_ref, 0, False)

    @pl.loop(0, LISTS)
    def _(k):
        j = lax.rem(mine + k, LISTS)

        @pl.loop(0, groups_of(count_ref[0, j]))
        def _(g):
            copy(j, g).start()

    @pl.loop(0, PANEL_BLK)
    def _(k):
        panel[k] = jnp.zeros((BS, F), jnp.float32)

    add_list(panel, own_ref, vals, count_ref, rows_ref, cols_ref, mine, lambda g: copy(mine, g).wait())

    @pl.loop(1, LISTS)
    def _(k):
        j = lax.rem(mine + k, LISTS)

        @pl.loop(0, groups_of(count_ref[0, j]))
        def _(g):
            copy(j, g).wait()


def more_products(pieces, split, *refs):
    place_ref, count_ref, rows_ref, cols_ref = refs[:4]
    vals = refs[5]
    panel = refs[6 + len(pieces) + 2 * len(split)]
    for (shift, flip), piece in zip(pieces, refs[6:]):
        add_list(panel, piece, vals, count_ref, rows_ref, cols_ref, piece_of(place_ref, shift, flip))
    if split:
        whole = refs[-1]
        rest = refs[6 + len(pieces) :]
        for i, (shift, flip) in enumerate(split):
            whole[:HALF, :] = rest[2 * i][...]
            whole[HALF:, :] = rest[2 * i + 1][...]
            add_list(panel, whole, vals, count_ref, rows_ref, cols_ref, piece_of(place_ref, shift, flip))


def quantize(block):
    peak = jnp.maximum(jnp.max(jnp.abs(block), axis=0, keepdims=True), 1e-32)
    exponent = jnp.ceil(jnp.log2(peak) + 0.001)
    scaled = block * (jnp.exp2(-exponent) * TOP)
    return jnp.round(scaled).astype(jnp.int32).astype(jnp.int16), exponent


def write_message(out_ref, index, blocks):
    count = len(blocks)
    row = lax.broadcasted_iota(jnp.int32, (16, F), 0)
    tail = jnp.zeros((16, F), jnp.float32)
    for i, block in enumerate(blocks):
        whole, exponent = quantize(block)
        out_ref[index, i * BS : (i + 1) * BS, :] = whole
        tail = jnp.where(row == i, exponent, tail)
    out_ref[index, count * BS : count * BS + 16, :] = tail.astype(jnp.int32).astype(jnp.int16)


def read_message(ref, index, count):
    tail = ref[index, count * BS : count * BS + 16, :].astype(jnp.int32).astype(jnp.float32)
    size = jnp.exp2(tail) * (1.0 / TOP)
    blocks = []
    for i in range(count):
        whole = ref[index, i * BS : (i + 1) * BS, :].astype(jnp.int32).astype(jnp.float32)
        blocks.append(whole * size[i : i + 1, :])
    return blocks


def add(first, *others):
    for other in others:
        first = [a + b for a, b in zip(first, other)]
    return first


class Here:
    def __init__(self, place_ref, panel=None):
        self.core, self.x, self.z = place_ref[2], place_ref[3], place_ref[4]
        self.panel = panel

    def x_of(self, other):
        return 1 - self.x if other else self.x

    def z_of(self, shift):
        return lax.rem(self.z + shift + 8, 8)

    def partial(self, other_x, z, part, other_core=False):
        core = 1 - self.core if other_core else self.core
        owner = self.x_of(other_x) * 16 + z * 2 + core
        return [self.panel[owner * PIECE_BLK + part[0] + i] for i in range(part[1])]


def core_messages(part, other_x, place_ref, panel, out_ref):
    here = Here(place_ref, panel)
    for k, other in enumerate(other_x):

        @pl.loop(0, 8)
        def _(z):
            write_message(out_ref, k * 8 + z, here.partial(other, z, part, other_core=True))


def last_products(pieces, split, *refs):
    more_products(pieces, split, *refs[:-2], refs[-1])
    core_messages(FIRST, (True,), refs[0], refs[-3], refs[-2])


def x_messages(place_ref, panel, rc_ref, out_ref):
    here = Here(place_ref, panel)

    @pl.loop(0, 8)
    def _(z):
        write_message(out_ref, z, add(here.partial(True, z, FIRST), read_message(rc_ref, z, FIRST[1])))


def base_value(part, here, rc_ref, rx_ref, other, z):
    if part == FIRST:
        return add(
            here.partial(other, z, part), read_message(rc_ref, z, part[1]), read_message(rx_ref, z, part[1])
        )
    return add(here.partial(other, z, part), read_message(rc_ref, other * 8 + z, part[1]))


def sides(part):
    return (0,) if part == FIRST else (0, 1)


def z_start(part, place_ref, panel, rc_ref, rx_ref, down_ref, up_ref):
    here = Here(place_ref, panel)
    for other in sides(part):
        for k, shift in enumerate((-4, -2)):
            write_message(
                down_ref, 2 * other + k, base_value(part, here, rc_ref, rx_ref, other, here.z_of(shift))
            )
        write_message(up_ref, other, base_value(part, here, rc_ref, rx_ref, other, here.z_of(2)))


def z_middle(part, place_ref, panel, rc_ref, rx_ref, down_ref, up_ref, three_ref, one_ref, back_ref, far_ref):
    here = Here(place_ref, panel)
    count = part[1]
    for other in sides(part):
        value = functools.partial(base_value, part, here, rc_ref, rx_ref, other)
        write_message(
            three_ref, other, add(value(here.z_of(-3)), read_message(down_ref, 2 * other, count))
        )
        write_message(far_ref, other, value(here.z_of(3)))
        write_message(
            one_ref, other, add(value(here.z_of(-1)), read_message(down_ref, 2 * other + 1, count))
        )
        write_message(back_ref, other, add(value(here.z_of(1)), read_message(up_ref, other, count)))


def z_end(place_ref, panel, rc_ref, *refs):
    here = Here(place_ref, panel)
    value = base_value(SECOND, here, rc_ref, None, 1, here.z)
    write_message(refs[4], 0, add(value, *[read_message(ref, 1, SECOND[1]) for ref in refs[:4]]))


def layer(place_ref, panel, rc1_ref, rx1_ref, rc2_ref, rx2_ref, *refs):
    here = Here(place_ref, panel)
    weight_ref, out_ref = refs[8], refs[9]
    first = base_value(FIRST, here, rc1_ref, rx1_ref, 0, here.z)
    first = add(first, *[read_message(ref, 0, FIRST[1]) for ref in refs[:4]])
    second = base_value(SECOND, here, rc2_ref, None, 0, here.z)
    second = add(second, read_message(rx2_ref, 0, 1), *[read_message(ref, 0, SECOND[1]) for ref in refs[4:8]])
    weight = weight_ref[...]
    for i, block in enumerate(first + second):
        high = block.astype(jnp.bfloat16)
        rest = block - high.astype(jnp.float32)
        middle = rest.astype(jnp.bfloat16)
        low = (rest - middle.astype(jnp.float32)).astype(jnp.bfloat16)
        result = jnp.dot(low, weight, preferred_element_type=jnp.float32)
        result += jnp.dot(middle, weight, preferred_element_type=jnp.float32)
        result += jnp.dot(high, weight, preferred_element_type=jnp.float32)
        out_ref[i * BS : (i + 1) * BS, :] = jnp.maximum(result, 0.0).astype(jnp.bfloat16)


def messages(count, part):
    return jax.ShapeDtypeStruct((count, message_rows(part[1]), F), jnp.int16)


def send_blk(array, dy, flip=0):
    pairs = [(y * 2 + h, ((y + dy) % 4) * 2 + (h ^ flip)) for y in range(4) for h in range(2)]
    return lax.ppermute(array, "blk", pairs)


def send_rep(array, dx, dz, dc):
    pairs = [
        (x * 16 + z * 2 + c, (x ^ dx) * 16 + ((z + dz) % 8) * 2 + (c ^ dc))
        for x in range(2) for z in range(8) for c in range(2)
    ]
    return lax.ppermute(array, "rep", pairs)


def sum_along_z(part, name, place, panel, rc, rx, also=None):
    count = len(sides(part))
    have = (rc,) if rx is None else (rc, rx)

    def fill(kernel):
        if rx is not None:
            return functools.partial(kernel, part)
        return lambda place_ref, panel_ref, rc_ref, *refs: kernel(part, place_ref, panel_ref, rc_ref, None, *refs)

    down, up = call(
        fill(z_start), name + "_start", (messages(2 * count, part), messages(count, part)),
        [SMEM] + [VMEM] * (1 + len(have)), (VMEM, VMEM), (place, panel, *have), 0.6,
    )
    down, up = send_rep(down, 0, -1, 0), send_rep(up, 0, 1, 0)
    down, also = lax.optimization_barrier((down, also))
    three, one, back, far = call(
        fill(z_middle), name + "_middle", (messages(count, part),) * 4,
        [SMEM] + [VMEM] * (3 + len(have)), (VMEM,) * 4, (place, panel, *have, down, up), 0.6,
    )
    arrived = send_rep(three, 0, -3, 0), send_rep(far, 0, 3, 0), send_rep(one, 0, -1, 0), send_rep(back, 0, 1, 0)
    return arrived, also


def local(node_feats, block_vals, block_rows, block_cols, block_count, weight):
    blk = lax.axis_index("blk")
    rep = lax.axis_index("rep")
    place = jnp.stack([blk // 2, blk % 2, rep % 2, rep // 16, (rep // 2) % 8]).astype(jnp.int32)
    lists = (place, block_count.reshape(1, LISTS), block_rows.reshape(LISTS, SLOTS), block_cols.reshape(LISTS, SLOTS))
    panel_type = jax.ShapeDtypeStruct((PANEL_BLK + 1, BS, F), jnp.float32)
    vals_type = jax.ShapeDtypeStruct((LISTS * SLOTS, BS, BS), jnp.bfloat16)
    piece_buffer = pltpu.VMEM((PIECE_ROWS, F), jnp.bfloat16)

    own = node_feats
    flipped, below, above = send_blk(own, 0, 1), send_blk(own, 1), send_blk(own, -1)
    panel, vals = call(
        first_products, "products_own", (panel_type, vals_type), [SMEM] * 4 + [VMEM, ANY], (VMEM, VMEM),
        (*lists, own, block_vals.reshape(LISTS * SLOTS, BS, BS)), 5, 40,
        scratch_shapes=[pltpu.SemaphoreType.DMA((LISTS * GROUPS,))],
    )

    def add_pieces(panel, name, which, arrays, split=(), kernel=more_products, extra=()):
        return call(
            functools.partial(kernel, which, split), name, (panel_type, *extra),
            [SMEM] * 4 + [VMEM] * (2 + len(arrays)), (VMEM,) * (1 + len(extra)), (*lists, panel, vals, *arrays), 3, 40,
            input_output_aliases={4: 0},
            scratch_shapes=[piece_buffer] if split else [],
        )

    panel, flipped, below, above = lax.optimization_barrier((panel, flipped, below, above))
    below_flipped, above_flipped = send_blk(flipped, 1), send_blk(flipped, -1)
    far = send_blk(below[:HALF], 1), send_blk(above[HALF:], -1)
    (panel,) = add_pieces(
        panel, "products_near", ((0, True), (3, False), (1, False)), (flipped, below, above)
    )
    panel, below_flipped, above_flipped = lax.optimization_barrier((panel, below_flipped, above_flipped))
    far_flipped = send_blk(below_flipped[:HALF], 1), send_blk(above_flipped[HALF:], -1)
    (panel,) = add_pieces(
        panel, "products_near_flipped", ((3, True), (1, True)), (below_flipped, above_flipped, *far), ((2, False),)
    )
    panel, to_core = add_pieces(
        panel, "products_far", (), far_flipped, ((2, True),), last_products, (messages(8, FIRST),)
    )

    def to_other_core(name, part, other_x):
        return call(
            functools.partial(core_messages, part, other_x), name, messages(8 * len(other_x), part),
            [SMEM, VMEM], VMEM, (place, panel), 0.6,
        )

    rc_cross = send_rep(to_core, 0, 0, 1)
    rc_second = send_rep(to_other_core("core_second", SECOND, (False, True)), 0, 0, 1)
    rc_first = send_rep(to_other_core("core_first", FIRST, (False,)), 0, 0, 1)
    to_x = call(x_messages, "x_first", messages(8, FIRST), [SMEM, VMEM, VMEM], VMEM, (place, panel, rc_cross), 0.6)
    rx_first = send_rep(to_x, 1, 0, 0)
    second, rc_first = sum_along_z(SECOND, "second", place, panel, rc_second, None, rc_first)
    to_x = call(
        z_end, "x_second", messages(1, SECOND), [SMEM] + [VMEM] * 6, VMEM, (place, panel, rc_second, *second), 0.6
    )
    panel, to_x = lax.optimization_barrier((panel, to_x))
    rx_second = send_rep(to_x, 1, 0, 0)
    first, _ = sum_along_z(FIRST, "first", place, panel, rc_first, rx_first)
    return call(
        layer, "layer", jax.ShapeDtypeStruct((PIECE_ROWS, H), jnp.bfloat16), [SMEM] + [VMEM] * 14, VMEM,
        (place, panel, rc_first, rx_first, rc_second, rx_second, *first, *second, weight), 1.5,
    )


def solution(mesh):
    return jax.shard_map(
        local,
        mesh=mesh,
        in_specs=(
            P(("blk", "rep"), None),
            P("blk", "rep", None, None, None, None),
            P("blk", "rep", None, None),
            P("blk", "rep", None, None),
            P("blk", "rep", None),
            P(),
        ),
        out_specs=P(("blk", "rep"), None),
        check_vma=False,
    )
```

```python
import functools

import jax
import jax.numpy as jnp
from jax import lax
from jax.experimental import pallas as pl
from jax.experimental.pallas import tpu as pltpu
from jax.sharding import PartitionSpec as P

BS = 128
F = 128
H = 256
SLOTS = 40
LISTS = 8
PIECE_BLK = 3
PIECE_ROWS = PIECE_BLK * BS
HALF = PIECE_ROWS // 2
PANEL_BLK = 96
GROUP = 8
GROUPS = SLOTS // GROUP
TOP = 32766.0
MIB = 1 << 20

FIRST, SECOND = (0, 2), (2, 1)


def message_rows(blocks):
    return blocks * BS + 16


SMEM = pl.BlockSpec(memory_space=pltpu.SMEM)
VMEM = pl.BlockSpec(memory_space=pltpu.VMEM)
ANY = pl.BlockSpec(memory_space=pl.ANY)


def call(kernel, name, out_shape, in_specs, out_specs, args, us, mib=24, **more):
    return pl.pallas_call(
        kernel,
        out_shape=out_shape,
        in_specs=in_specs,
        out_specs=out_specs,
        compiler_params=pltpu.CompilerParams(vmem_limit_bytes=mib * MIB),
        cost_estimate=pl.CostEstimate(flops=0, bytes_accessed=int(us * 3.0e6), transcendentals=0),
        name=name,
        **more,
    )(*args)


def groups_of(count):
    return lax.div(jnp.clip(count, 0, SLOTS) + (GROUP - 1), GROUP)


def fetch(vals_ref, vals, sems, count_ref, j, k):
    def each(action):
        @pl.loop(0, groups_of(count_ref[0, j]))
        def _(g):
            action(
                pltpu.make_async_copy(
                    vals_ref.at[pl.ds(pl.multiple_of(j * SLOTS + g * GROUP, GROUP), GROUP)],
                    vals.at[pl.ds(pl.multiple_of(k * SLOTS + g * GROUP, GROUP), GROUP)],
                    sems.at[k * GROUPS + g],
                )
            )

    return each


def add_list(panel, piece, vals, count_ref, lists_ref, j, k, wait=None):
    count = count_ref[0, j]

    @pl.loop(0, groups_of(count))
    def _(g):
        if wait is not None:
            wait(g)
        products, rows = [], []
        for u in range(GROUP):
            q = g * GROUP + u
            entry = jnp.where(q < count, lists_ref[j, q], PANEL_BLK * 4)
            rows.append(entry >> 2)
            products.append(
                jnp.dot(
                    vals[k * SLOTS + q],
                    piece[pl.ds(pl.multiple_of((entry & 3) * BS, BS), BS), :],
                    preferred_element_type=jnp.float32,
                )
            )
        for row, product in zip(rows, products):
            panel[row] += product


def group_wait(vals_ref, vals, sems, j, k):
    def wait(g):
        pltpu.make_async_copy(
            vals_ref.at[pl.ds(pl.multiple_of(j * SLOTS + g * GROUP, GROUP), GROUP)],
            vals.at[pl.ds(pl.multiple_of(k * SLOTS + g * GROUP, GROUP), GROUP)],
            sems.at[k * GROUPS + g],
        ).wait()

    return wait


def piece_of(place_ref, shift, flip):
    x_hi = place_ref[1]
    return lax.rem(place_ref[0] + shift, 4) * 2 + (1 - x_hi if flip else x_hi)


def first_products(place_ref, count_ref, lists_ref, own_ref, vals_ref, panel, own, vals, sems, own_sem):
    mine = piece_of(place_ref, 0, False)
    own_copy = pltpu.make_async_copy(own_ref, own, own_sem)
    own_copy.start()
    fetch(vals_ref, vals, sems, count_ref, mine, 0)(lambda copy: copy.start())

    @pl.loop(0, PANEL_BLK // 4)
    def _(k):
        for u in range(4):
            panel[k * 4 + u] = jnp.zeros((BS, F), jnp.float32)

    own_copy.wait()
    add_list(panel, own, vals, count_ref, lists_ref, mine, 0, group_wait(vals_ref, vals, sems, mine, 0))


def more_products(pieces, split, ahead, *refs):
    place_ref, count_ref, lists_ref, _, vals_ref = refs[:5]
    inputs = 5 + len(pieces) + 2 * len(split)
    arrays, outputs = refs[5:inputs], refs[inputs:]
    panel = outputs[0]
    vals, sems, whole = outputs[-3:]
    todo = [piece_of(place_ref, *which) for which in pieces + split]
    for k, j in enumerate(todo):
        fetch(vals_ref, vals, sems, count_ref, j, k)(lambda copy: copy.start())
    if ahead:
        next_vals, next_sems = outputs[1], outputs[2]
        later = fetch(vals_ref, next_vals, next_sems, count_ref, piece_of(place_ref, *ahead), 0)
        later(lambda copy: copy.start())
    for k, j in enumerate(todo):
        piece = whole
        if k < len(pieces):
            piece = arrays[k]
        else:
            first = len(pieces) + 2 * (k - len(pieces))
            whole[:HALF, :] = arrays[first][...]
            whole[HALF:, :] = arrays[first + 1][...]
        add_list(panel, piece, vals, count_ref, lists_ref, j, k, group_wait(vals_ref, vals, sems, j, k))
    if ahead:
        later(lambda copy: copy.wait())


def quantize(block):
    peak = jnp.maximum(jnp.max(jnp.abs(block), axis=0, keepdims=True), 1e-32)
    exponent = jnp.ceil(jnp.log2(peak) + 0.001)
    scaled = block * (jnp.exp2(-exponent) * TOP)
    return jnp.round(scaled).astype(jnp.int32).astype(jnp.int16), exponent


def write_message(out_ref, index, blocks):
    count = len(blocks)
    row = lax.broadcasted_iota(jnp.int32, (16, F), 0)
    tail = jnp.zeros((16, F), jnp.float32)
    for i, block in enumerate(blocks):
        whole, exponent = quantize(block)
        out_ref[index, i * BS : (i + 1) * BS, :] = whole
        tail = jnp.where(row == i, exponent, tail)
    out_ref[index, count * BS : count * BS + 16, :] = tail.astype(jnp.int32).astype(jnp.int16)


def read_message(ref, index, count):
    tail = ref[index, count * BS : count * BS + 16, :].astype(jnp.int32).astype(jnp.float32)
    size = jnp.exp2(tail) * (1.0 / TOP)
    blocks = []
    for i in range(count):
        whole = ref[index, i * BS : (i + 1) * BS, :].astype(jnp.int32).astype(jnp.float32)
        blocks.append(whole * size[i : i + 1, :])
    return blocks


def add(first, *others):
    for other in others:
        first = [a + b for a, b in zip(first, other)]
    return first


class Here:
    def __init__(self, place_ref, panel=None):
        self.core, self.x, self.z = place_ref[2], place_ref[3], place_ref[4]
        self.panel = panel

    def x_of(self, other):
        return 1 - self.x if other else self.x

    def z_of(self, shift):
        return lax.rem(self.z + shift + 8, 8)

    def partial(self, other_x, z, part, other_core=False):
        core = 1 - self.core if other_core else self.core
        owner = self.x_of(other_x) * 16 + z * 2 + core
        return [self.panel[owner * PIECE_BLK + part[0] + i] for i in range(part[1])]


def core_messages(part, other_x, place_ref, panel, out_ref):
    here = Here(place_ref, panel)
    for k, other in enumerate(other_x):

        @pl.loop(0, 8)
        def _(z):
            write_message(out_ref, k * 8 + z, here.partial(other, z, part, other_core=True))


def last_products(which, place_ref, count_ref, lists_ref, _, vals, top_ref, bottom_ref, panel, out_ref, whole):
    whole[:HALF, :] = top_ref[...]
    whole[HALF:, :] = bottom_ref[...]
    add_list(panel, whole, vals, count_ref, lists_ref, piece_of(place_ref, *which), 0)
    core_messages(FIRST, (True,), place_ref, panel, out_ref)


def x_messages(place_ref, panel, rc_ref, out_ref):
    here = Here(place_ref, panel)

    @pl.loop(0, 8)
    def _(z):
        write_message(out_ref, z, add(here.partial(True, z, FIRST), read_message(rc_ref, z, FIRST[1])))


def base_value(part, here, rc_ref, rx_ref, other, z):
    if part == FIRST:
        return add(
            here.partial(other, z, part), read_message(rc_ref, z, part[1]), read_message(rx_ref, z, part[1])
        )
    return add(here.partial(other, z, part), read_message(rc_ref, other * 8 + z, part[1]))


def sides(part):
    return (0,) if part == FIRST else (0, 1)


def z_start(part, place_ref, panel, rc_ref, rx_ref, down_ref, up_ref, two_ref, far_ref):
    here = Here(place_ref, panel)
    for other in sides(part):
        for out_ref, index, shift in (
            (down_ref, 2 * other, -4), (down_ref, 2 * other + 1, -1), (up_ref, other, 2),
            (two_ref, other, -2), (far_ref, other, 3),
        ):
            write_message(out_ref, index, base_value(part, here, rc_ref, rx_ref, other, here.z_of(shift)))


def z_middle(part, place_ref, panel, rc_ref, rx_ref, down_ref, up_ref, three_ref, one_ref):
    here = Here(place_ref, panel)
    count = part[1]
    for other in sides(part):
        value = functools.partial(base_value, part, here, rc_ref, rx_ref, other)
        write_message(three_ref, other, add(value(here.z_of(-3)), read_message(down_ref, 2 * other, count)))
        write_message(one_ref, other, add(value(here.z_of(1)), read_message(up_ref, other, count)))


def arrivals(part, other, down_ref, *refs):
    return [read_message(down_ref, 2 * other + 1, part[1])] + [read_message(ref, other, part[1]) for ref in refs]


def z_end(place_ref, panel, rc_ref, *refs):
    here = Here(place_ref, panel)
    value = base_value(SECOND, here, rc_ref, None, 1, here.z)
    write_message(refs[5], 0, add(value, *arrivals(SECOND, 1, *refs[:5])))


def layer(place_ref, panel, rc1_ref, rx1_ref, rc2_ref, rx2_ref, *refs):
    here = Here(place_ref, panel)
    weight_ref, out_ref = refs[10], refs[11]
    first = base_value(FIRST, here, rc1_ref, rx1_ref, 0, here.z)
    first = add(first, *arrivals(FIRST, 0, *refs[:5]))
    second = base_value(SECOND, here, rc2_ref, None, 0, here.z)
    second = add(second, read_message(rx2_ref, 0, 1), *arrivals(SECOND, 0, *refs[5:10]))
    weight = weight_ref[...]
    for i, block in enumerate(first + second):
        high = block.astype(jnp.bfloat16)
        rest = block - high.astype(jnp.float32)
        middle = rest.astype(jnp.bfloat16)
        low = (rest - middle.astype(jnp.float32)).astype(jnp.bfloat16)
        result = jnp.dot(low, weight, preferred_element_type=jnp.float32)
        result += jnp.dot(middle, weight, preferred_element_type=jnp.float32)
        result += jnp.dot(high, weight, preferred_element_type=jnp.float32)
        out_ref[i * BS : (i + 1) * BS, :] = jnp.maximum(result, 0.0).astype(jnp.bfloat16)


def messages(count, part):
    return jax.ShapeDtypeStruct((count, message_rows(part[1]), F), jnp.int16)


def send_blk(array, dy, flip=0):
    pairs = [(y * 2 + h, ((y + dy) % 4) * 2 + (h ^ flip)) for y in range(4) for h in range(2)]
    return lax.ppermute(array, "blk", pairs)


def send_rep(array, dx, dz, dc):
    pairs = [
        (x * 16 + z * 2 + c, (x ^ dx) * 16 + ((z + dz) % 8) * 2 + (c ^ dc))
        for x in range(2) for z in range(8) for c in range(2)
    ]
    return lax.ppermute(array, "rep", pairs)


def sum_along_z(part, name, place, panel, rc, rx, also=None):
    count = len(sides(part))
    have = (rc,) if rx is None else (rc, rx)

    def fill(kernel):
        if rx is not None:
            return functools.partial(kernel, part)
        return lambda place_ref, panel_ref, rc_ref, *refs: kernel(part, place_ref, panel_ref, rc_ref, None, *refs)

    down, up, two, far = call(
        fill(z_start), name + "_start", (messages(2 * count, part),) + (messages(count, part),) * 3,
        [SMEM] + [VMEM] * (1 + len(have)), (VMEM,) * 4, (place, panel, *have), 0.6,
    )
    down, up = send_rep(down, 0, -1, 0), send_rep(up, 0, 1, 0)
    two, far = send_rep(two, 0, -2, 0), send_rep(far, 0, 3, 0)
    down, also = lax.optimization_barrier((down, also))
    three, one = call(
        fill(z_middle), name + "_middle", (messages(count, part),) * 2,
        [SMEM] + [VMEM] * (3 + len(have)), (VMEM,) * 2, (place, panel, *have, down, up), 0.6,
    )
    return (down, two, far, send_rep(three, 0, -3, 0), send_rep(one, 0, 1, 0)), also


def local(node_feats, block_vals, block_rows, block_cols, block_count, weight):
    blk = lax.axis_index("blk")
    rep = lax.axis_index("rep")
    place = jnp.stack([blk // 2, blk % 2, rep % 2, rep // 16, (rep // 2) % 8]).astype(jnp.int32)
    slots = block_rows.reshape(LISTS, SLOTS) * 4 + block_cols.reshape(LISTS, SLOTS)
    lists = (place, block_count.reshape(1, LISTS), slots)
    vals = block_vals.reshape(LISTS * SLOTS, BS, BS)
    panel_type = jax.ShapeDtypeStruct((PANEL_BLK + 1, BS, F), jnp.float32)
    list_type = jax.ShapeDtypeStruct((SLOTS, BS, BS), jnp.bfloat16)
    piece_buffer = pltpu.VMEM((PIECE_ROWS, F), jnp.bfloat16)

    def list_buffers(count):
        return [pltpu.VMEM((count * SLOTS, BS, BS), jnp.bfloat16), pltpu.SemaphoreType.DMA((count * GROUPS,))]

    own = node_feats
    flipped, below, above = send_blk(own, 0, 1), send_blk(own, 1), send_blk(own, -1)
    panel = call(
        first_products, "products_own", panel_type, [SMEM] * 3 + [ANY] * 2, VMEM, (*lists, own, vals), 3, 41,
        scratch_shapes=[piece_buffer, *list_buffers(1), pltpu.SemaphoreType.DMA],
    )
    panel, flipped, below, above = lax.optimization_barrier((panel, flipped, below, above))
    below_flipped, above_flipped = send_blk(flipped, 1), send_blk(flipped, -1)
    far = send_blk(below[:HALF], 1), send_blk(above[HALF:], -1)
    panel = call(
        functools.partial(more_products, ((0, True), (3, False), (1, False)), (), None), "products_near", panel_type,
        [SMEM] * 3 + [VMEM, ANY] + [VMEM] * 3, VMEM, (*lists, panel, vals, flipped, below, above), 4, 41,
        input_output_aliases={3: 0},
        scratch_shapes=[*list_buffers(3), piece_buffer],
    )
    panel, below_flipped, above_flipped, far = lax.optimization_barrier((panel, below_flipped, above_flipped, far))
    far_flipped = send_blk(below_flipped[:HALF], 1), send_blk(above_flipped[HALF:], -1)
    panel, last_vals = call(
        functools.partial(more_products, ((3, True), (1, True)), ((2, False),), (2, True)),
        "products_near_flipped", (panel_type, list_type),
        [SMEM] * 3 + [VMEM, ANY] + [VMEM] * 4, (VMEM,) * 2,
        (*lists, panel, vals, below_flipped, above_flipped, *far), 3, 41,
        input_output_aliases={3: 0},
        scratch_shapes=[pltpu.SemaphoreType.DMA((GROUPS,)), *list_buffers(3), piece_buffer],
    )
    panel, to_core = call(
        functools.partial(last_products, (2, True)), "products_far", (panel_type, messages(8, FIRST)),
        [SMEM] * 3 + [VMEM] * 4, (VMEM,) * 2, (*lists, panel, last_vals, *far_flipped), 3, 40,
        input_output_aliases={3: 0},
        scratch_shapes=[piece_buffer],
    )

    def to_other_core(name, part, other_x):
        return call(
            functools.partial(core_messages, part, other_x), name, messages(8 * len(other_x), part),
            [SMEM, VMEM], VMEM, (place, panel), 0.6,
        )

    rc_cross = send_rep(to_core, 0, 0, 1)
    rc_second = send_rep(to_other_core("core_second", SECOND, (False, True)), 0, 0, 1)
    rc_first = send_rep(to_other_core("core_first", FIRST, (False,)), 0, 0, 1)
    to_x = call(x_messages, "x_first", messages(8, FIRST), [SMEM, VMEM, VMEM], VMEM, (place, panel, rc_cross), 0.6)
    rx_first = send_rep(to_x, 1, 0, 0)
    second, rc_first = sum_along_z(SECOND, "second", place, panel, rc_second, None, rc_first)
    to_x = call(
        z_end, "x_second", messages(1, SECOND), [SMEM] + [VMEM] * 7, VMEM, (place, panel, rc_second, *second), 0.6
    )
    panel, to_x = lax.optimization_barrier((panel, to_x))
    rx_second = send_rep(to_x, 1, 0, 0)
    first, _ = sum_along_z(FIRST, "first", place, panel, rc_first, rx_first)
    return call(
        layer, "layer", jax.ShapeDtypeStruct((PIECE_ROWS, H), jnp.bfloat16), [SMEM] + [VMEM] * 16, VMEM,
        (place, panel, rc_first, rx_first, rc_second, rx_second, *first, *second, weight), 1.5,
    )


def solution(mesh):
    return jax.shard_map(
        local,
        mesh=mesh,
        in_specs=(
            P(("blk", "rep"), None),
            P("blk", "rep", None, None, None, None),
            P("blk", "rep", None, None),
            P("blk", "rep", None, None),
            P("blk", "rep", None),
            P(),
        ),
        out_specs=P(("blk", "rep"), None),
        check_vma=False,
    )
```

```python
import functools

import jax
import jax.numpy as jnp
from jax import lax
from jax.experimental import pallas as pl
from jax.experimental.pallas import tpu as pltpu
from jax.sharding import PartitionSpec as P

BS = 128
F = 128
H = 256
SLOTS = 40
LISTS = 8
PIECE_BLK = 3
PIECE_ROWS = PIECE_BLK * BS
HALF = PIECE_ROWS // 2
PANEL_BLK = 96
GROUP = 8
GROUPS = SLOTS // GROUP
TOP = 32766.0
MIB = 1 << 20

FIRST, SECOND = (0, 2), (2, 1)


def message_rows(blocks):
    return blocks * BS + 16


SMEM = pl.BlockSpec(memory_space=pltpu.SMEM)
VMEM = pl.BlockSpec(memory_space=pltpu.VMEM)
ANY = pl.BlockSpec(memory_space=pl.ANY)


def call(kernel, name, out_shape, in_specs, out_specs, args, us, mib=24, **more):
    return pl.pallas_call(
        kernel,
        out_shape=out_shape,
        in_specs=in_specs,
        out_specs=out_specs,
        compiler_params=pltpu.CompilerParams(vmem_limit_bytes=mib * MIB),
        cost_estimate=pl.CostEstimate(flops=0, bytes_accessed=int(us * 3.0e6), transcendentals=0),
        name=name,
        **more,
    )(*args)


def groups_of(count):
    return lax.div(jnp.clip(count, 0, SLOTS) + (GROUP - 1), GROUP)


def fetch(vals_ref, vals, sems, count_ref, j, k):
    def each(action):
        @pl.loop(0, groups_of(count_ref[0, j]))
        def _(g):
            action(
                pltpu.make_async_copy(
                    vals_ref.at[pl.ds(pl.multiple_of(j * SLOTS + g * GROUP, GROUP), GROUP)],
                    vals.at[pl.ds(pl.multiple_of(k * SLOTS + g * GROUP, GROUP), GROUP)],
                    sems.at[k * GROUPS + g],
                )
            )

    return each


def add_list(panel, piece, vals, count_ref, lists_ref, j, k, wait=None):
    count = count_ref[0, j]

    @pl.loop(0, groups_of(count))
    def _(g):
        if wait is not None:
            wait(g)
        products, rows = [], []
        for u in range(GROUP):
            q = g * GROUP + u
            entry = jnp.where(q < count, lists_ref[j, q], PANEL_BLK * 4)
            rows.append(entry >> 2)
            products.append(
                jnp.dot(
                    vals[k * SLOTS + q],
                    piece[pl.ds(pl.multiple_of((entry & 3) * BS, BS), BS), :],
                    preferred_element_type=jnp.float32,
                )
            )
        for row, product in zip(rows, products):
            panel[row] += product


def group_wait(vals_ref, vals, sems, j, k):
    def wait(g):
        pltpu.make_async_copy(
            vals_ref.at[pl.ds(pl.multiple_of(j * SLOTS + g * GROUP, GROUP), GROUP)],
            vals.at[pl.ds(pl.multiple_of(k * SLOTS + g * GROUP, GROUP), GROUP)],
            sems.at[k * GROUPS + g],
        ).wait()

    return wait


def piece_of(place_ref, shift, flip):
    x_hi = place_ref[1]
    return lax.rem(place_ref[0] + shift, 4) * 2 + (1 - x_hi if flip else x_hi)


def first_products(place_ref, count_ref, lists_ref, own_ref, vals_ref, panel, own, vals, sems, own_sem):
    mine = piece_of(place_ref, 0, False)
    own_copy = pltpu.make_async_copy(own_ref, own, own_sem)
    own_copy.start()
    fetch(vals_ref, vals, sems, count_ref, mine, 0)(lambda copy: copy.start())

    @pl.loop(0, PANEL_BLK // 4)
    def _(k):
        for u in range(4):
            panel[k * 4 + u] = jnp.zeros((BS, F), jnp.float32)

    own_copy.wait()
    add_list(panel, own, vals, count_ref, lists_ref, mine, 0, group_wait(vals_ref, vals, sems, mine, 0))


def more_products(pieces, ahead, place_ref, count_ref, lists_ref, _, vals_ref, *refs):
    inputs = 1 + max(array for _, (array, _) in pieces)
    pairs, (panel, *outputs) = refs[:inputs], refs[inputs:]
    vals, sems = outputs[-2:]
    todo = [piece_of(place_ref, *which) for which, _ in pieces]
    for k, j in enumerate(todo):
        fetch(vals_ref, vals, sems, count_ref, j, k)(lambda copy: copy.start())
    later = [
        fetch(vals_ref, outputs[0], outputs[1], count_ref, piece_of(place_ref, *which), k)
        for k, which in enumerate(ahead)
    ]
    for each in later:
        each(lambda copy: copy.start())
    for k, (j, (_, (array, half))) in enumerate(zip(todo, pieces)):
        add_list(
            panel, pairs[array].at[half], vals, count_ref, lists_ref, j, k,
            group_wait(vals_ref, vals, sems, j, k),
        )
    for each in later:
        each(lambda copy: copy.wait())


def quantize(block):
    peak = jnp.maximum(jnp.max(jnp.abs(block), axis=0, keepdims=True), 1e-32)
    exponent = jnp.ceil(jnp.log2(peak) + 0.001)
    scaled = block * (jnp.exp2(-exponent) * TOP)
    return jnp.round(scaled).astype(jnp.int32).astype(jnp.int16), exponent


def write_message(out_ref, index, blocks):
    count = len(blocks)
    row = lax.broadcasted_iota(jnp.int32, (16, F), 0)
    tail = jnp.zeros((16, F), jnp.float32)
    for i, block in enumerate(blocks):
        whole, exponent = quantize(block)
        out_ref[index, i * BS : (i + 1) * BS, :] = whole
        tail = jnp.where(row == i, exponent, tail)
    out_ref[index, count * BS : count * BS + 16, :] = tail.astype(jnp.int32).astype(jnp.int16)


def read_message(ref, index, count):
    tail = ref[index, count * BS : count * BS + 16, :].astype(jnp.int32).astype(jnp.float32)
    size = jnp.exp2(tail) * (1.0 / TOP)
    blocks = []
    for i in range(count):
        whole = ref[index, i * BS : (i + 1) * BS, :].astype(jnp.int32).astype(jnp.float32)
        blocks.append(whole * size[i : i + 1, :])
    return blocks


def add(first, *others):
    for other in others:
        first = [a + b for a, b in zip(first, other)]
    return first


class Here:
    def __init__(self, place_ref, panel=None):
        self.core, self.x, self.z = place_ref[2], place_ref[3], place_ref[4]
        self.panel = panel

    def x_of(self, other):
        return 1 - self.x if other else self.x

    def z_of(self, shift):
        return lax.rem(self.z + shift + 8, 8)

    def partial(self, other_x, z, part, other_core=False):
        core = 1 - self.core if other_core else self.core
        owner = self.x_of(other_x) * 16 + z * 2 + core
        return [self.panel[owner * PIECE_BLK + part[0] + i] for i in range(part[1])]


def core_messages(part, other_x, place_ref, panel, out_ref):
    here = Here(place_ref, panel)
    for k, other in enumerate(other_x):

        @pl.loop(0, 8)
        def _(z):
            write_message(out_ref, k * 8 + z, here.partial(other, z, part, other_core=True))


def last_products(pieces, place_ref, count_ref, lists_ref, _, vals, *refs):
    *arrays, panel, out_ref = refs
    for k, (which, piece) in enumerate(zip(pieces, arrays)):
        add_list(panel, piece, vals, count_ref, lists_ref, piece_of(place_ref, *which), k)
    core_messages(FIRST, (True,), place_ref, panel, out_ref)


def pair_up(first_ref, second_ref, out_ref):
    out_ref[0] = first_ref[...]
    out_ref[1] = second_ref[...]


def x_messages(place_ref, panel, rc_ref, out_ref):
    here = Here(place_ref, panel)

    @pl.loop(0, 8)
    def _(z):
        write_message(out_ref, z, add(here.partial(True, z, FIRST), read_message(rc_ref, z, FIRST[1])))


def base_value(part, here, rc_ref, rx_ref, other, z):
    value = add(here.partial(other, z, part), read_message(rc_ref, other * 8 + z, part[1]))
    return value if rx_ref is None else add(value, read_message(rx_ref, z, part[1]))


def sides(part):
    return (0,) if part == FIRST else (0, 1)


def z_start(part, place_ref, panel, rc_ref, rx_ref, relay_ref, down_ref, up_ref):
    here = Here(place_ref, panel)
    for other in sides(part):
        for out_ref, index, shift in (
            (relay_ref, other, -4), (down_ref, 2 * other, -3), (up_ref, 2 * other, 3),
            (down_ref, 2 * other + 1, -1), (up_ref, 2 * other + 1, 1),
        ):
            write_message(out_ref, index, base_value(part, here, rc_ref, rx_ref, other, here.z_of(shift)))


def z_middle(part, place_ref, panel, rc_ref, rx_ref, relay_ref, down_ref, up_ref, below_ref, above_ref):
    here = Here(place_ref, panel)
    count = part[1]
    for other in sides(part):
        value = functools.partial(base_value, part, here, rc_ref, rx_ref, other)
        come = add(read_message(relay_ref, other, count), read_message(down_ref, 2 * other, count))
        write_message(below_ref, other, add(value(here.z_of(-2)), come))
        write_message(above_ref, other, add(value(here.z_of(2)), read_message(up_ref, 2 * other, count)))


def arrivals(part, other, down_ref, up_ref, below_ref, above_ref):
    straight = [read_message(ref, 2 * other + 1, part[1]) for ref in (down_ref, up_ref)]
    return straight + [read_message(ref, other, part[1]) for ref in (below_ref, above_ref)]


def z_end(place_ref, panel, rc_ref, *refs):
    here = Here(place_ref, panel)
    *arrived, out_ref, sum_ref = refs
    value = base_value(SECOND, here, rc_ref, None, 1, here.z)
    write_message(out_ref, 0, add(value, *arrivals(SECOND, 1, *arrived)))
    value = base_value(SECOND, here, rc_ref, None, 0, here.z)
    sum_ref[...] = add(value, *arrivals(SECOND, 0, *arrived))[0]


def layer(place_ref, panel, rc_ref, rx_ref, sum_ref, rx2_ref, *refs):
    here = Here(place_ref, panel)
    *arrived, weight_ref, out_ref = refs
    first = add(base_value(FIRST, here, rc_ref, rx_ref, 0, here.z), *arrivals(FIRST, 0, *arrived))
    second = add([sum_ref[...]], read_message(rx2_ref, 0, SECOND[1]))
    weight = weight_ref[...]
    for i, block in enumerate(first + second):
        high = block.astype(jnp.bfloat16)
        rest = block - high.astype(jnp.float32)
        middle = rest.astype(jnp.bfloat16)
        low = (rest - middle.astype(jnp.float32)).astype(jnp.bfloat16)
        result = jnp.dot(low, weight, preferred_element_type=jnp.float32)
        result += jnp.dot(middle, weight, preferred_element_type=jnp.float32)
        result += jnp.dot(high, weight, preferred_element_type=jnp.float32)
        out_ref[i * BS : (i + 1) * BS, :] = jnp.maximum(result, 0.0).astype(jnp.bfloat16)


def messages(count, part):
    return jax.ShapeDtypeStruct((count, message_rows(part[1]), F), jnp.int16)


def send_blk(array, dy, flip=0):
    pairs = [(y * 2 + h, ((y + dy) % 4) * 2 + (h ^ flip)) for y in range(4) for h in range(2)]
    return lax.ppermute(array, "blk", pairs)


def send_rep(array, dx, dz, dc):
    pairs = [
        (x * 16 + z * 2 + c, (x ^ dx) * 16 + ((z + dz) % 8) * 2 + (c ^ dc))
        for x in range(2) for z in range(8) for c in range(2)
    ]
    return lax.ppermute(array, "rep", pairs)


def sum_along_z(part, name, place, panel, rc, rx, also=None):
    count = len(sides(part))
    have = (rc,) if rx is None else (rc, rx)

    def fill(kernel):
        if rx is not None:
            return functools.partial(kernel, part)
        return lambda place_ref, panel_ref, rc_ref, *refs: kernel(part, place_ref, panel_ref, rc_ref, None, *refs)

    relay, down, up = call(
        fill(z_start), name + "_start", (messages(count, part), messages(2 * count, part), messages(2 * count, part)),
        [SMEM] + [VMEM] * (1 + len(have)), (VMEM,) * 3, (place, panel, *have), 0.6,
    )
    relay, down, up = send_rep(relay, 0, -2, 0), send_rep(down, 0, -1, 0), send_rep(up, 0, 1, 0)
    down, also = lax.optimization_barrier((down, also))
    below, above = call(
        fill(z_middle), name + "_middle", (messages(count, part),) * 2,
        [SMEM] + [VMEM] * (4 + len(have)), (VMEM,) * 2, (place, panel, *have, relay, down, up), 0.6,
    )
    return (down, up, send_rep(below, 0, -2, 0), send_rep(above, 0, 2, 0)), also


def local(node_feats, block_vals, block_rows, block_cols, block_count, weight):
    blk = lax.axis_index("blk")
    rep = lax.axis_index("rep")
    place = jnp.stack([blk // 2, blk % 2, rep % 2, rep // 16, (rep // 2) % 8]).astype(jnp.int32)
    slots = block_rows.reshape(LISTS, SLOTS) * 4 + block_cols.reshape(LISTS, SLOTS)
    lists = (place, block_count.reshape(1, LISTS), slots)
    vals = block_vals.reshape(LISTS * SLOTS, BS, BS)
    panel_type = jax.ShapeDtypeStruct((PANEL_BLK + 1, BS, F), jnp.float32)
    piece_buffer = pltpu.VMEM((PIECE_ROWS, F), jnp.bfloat16)

    def list_buffers(count):
        return [pltpu.VMEM((count * SLOTS, BS, BS), jnp.bfloat16), pltpu.SemaphoreType.DMA((count * GROUPS,))]

    own = node_feats
    flipped = send_blk(own, 0, 1)
    panel = call(
        first_products, "products_own", panel_type, [SMEM] * 3 + [ANY] * 2, VMEM, (*lists, own, vals), 3, 41,
        scratch_shapes=[piece_buffer, *list_buffers(1), pltpu.SemaphoreType.DMA],
    )
    panel, flipped = lax.optimization_barrier((panel, flipped))
    pair = call(
        pair_up, "pair", jax.ShapeDtypeStruct((2, PIECE_ROWS, F), jnp.bfloat16), [VMEM] * 2, VMEM, (own, flipped), 0.3
    )
    below, above = send_blk(pair, 1), send_blk(pair, -1)
    panel = call(
        functools.partial(more_products, (((0, True), (0, 1)),), ()), "products_flipped", panel_type,
        [SMEM] * 3 + [VMEM, ANY, VMEM], VMEM, (*lists, panel, vals, pair), 3, 41,
        input_output_aliases={3: 0},
        scratch_shapes=list_buffers(1),
    )
    panel, below, above = lax.optimization_barrier((panel, below, above))
    far = send_blk(below[0], 1), send_blk(above[1], -1)
    far_pieces = (2, False), (2, True)
    near_pieces = ((3, False), (0, 0)), ((3, True), (0, 1)), ((1, False), (1, 0)), ((1, True), (1, 1))
    panel, last_vals = call(
        functools.partial(more_products, near_pieces, far_pieces), "products_near",
        (panel_type, jax.ShapeDtypeStruct((2 * SLOTS, BS, BS), jnp.bfloat16)),
        [SMEM] * 3 + [VMEM, ANY] + [VMEM] * 2, (VMEM,) * 2, (*lists, panel, vals, below, above), 3, 41,
        input_output_aliases={3: 0},
        scratch_shapes=[pltpu.SemaphoreType.DMA((2 * GROUPS,)), *list_buffers(4)],
    )
    panel, to_core = call(
        functools.partial(last_products, far_pieces), "products_far", (panel_type, messages(8, FIRST)),
        [SMEM] * 3 + [VMEM] * 4, (VMEM,) * 2, (*lists, panel, last_vals, *far), 3, 40,
        input_output_aliases={3: 0},
    )

    def to_other_core(name, part, other_x):
        return call(
            functools.partial(core_messages, part, other_x), name, messages(8 * len(other_x), part),
            [SMEM, VMEM], VMEM, (place, panel), 0.6,
        )

    rc_cross = send_rep(to_core, 0, 0, 1)
    rc_second = send_rep(to_other_core("core_second", SECOND, (False, True)), 0, 0, 1)
    rc_first = send_rep(to_other_core("core_first", FIRST, (False,)), 0, 0, 1)
    to_x = call(x_messages, "x_first", messages(8, FIRST), [SMEM, VMEM, VMEM], VMEM, (place, panel, rc_cross), 0.6)
    rx_first = send_rep(to_x, 1, 0, 0)
    second, rc_first = sum_along_z(SECOND, "second", place, panel, rc_second, None, rc_first)
    to_x, own_sum = call(
        z_end, "x_second", (messages(1, SECOND), jax.ShapeDtypeStruct((BS, F), jnp.float32)),
        [SMEM] + [VMEM] * 6, (VMEM,) * 2, (place, panel, rc_second, *second), 0.6,
    )
    panel, to_x = lax.optimization_barrier((panel, to_x))
    rx_second = send_rep(to_x, 1, 0, 0)
    first, _ = sum_along_z(FIRST, "first", place, panel, rc_first, rx_first)
    return call(
        layer, "layer", jax.ShapeDtypeStruct((PIECE_ROWS, H), jnp.bfloat16), [SMEM] + [VMEM] * 10, VMEM,
        (place, panel, rc_first, rx_first, own_sum, rx_second, *first, weight), 1.5,
    )


def solution(mesh):
    return jax.shard_map(
        local,
        mesh=mesh,
        in_specs=(
            P(("blk", "rep"), None),
            P("blk", "rep", None, None, None, None),
            P("blk", "rep", None, None),
            P("blk", "rep", None, None),
            P("blk", "rep", None),
            P(),
        ),
        out_specs=P(("blk", "rep"), None),
        check_vma=False,
    )
```

```python
import functools

import jax
import jax.numpy as jnp
from jax import lax
from jax.experimental import pallas as pl
from jax.experimental.pallas import tpu as pltpu
from jax.sharding import PartitionSpec as P

BS = 128
F = 128
H = 256
SLOTS = 40
LISTS = 8
PIECE_BLK = 3
PIECE_ROWS = PIECE_BLK * BS
HALF = PIECE_ROWS // 2
PANEL_BLK = 96
GROUP = 8
GROUPS = SLOTS // GROUP
TOP = 32766.0
MIB = 1 << 20

FIRST, SECOND = (0, 144, 2), (288, 96, 1)


def message_rows(part):
    return part[1] * part[2] + 16


SMEM = pl.BlockSpec(memory_space=pltpu.SMEM)
VMEM = pl.BlockSpec(memory_space=pltpu.VMEM)
ANY = pl.BlockSpec(memory_space=pl.ANY)


def call(kernel, name, out_shape, in_specs, out_specs, args, us, mib=24, **more):
    return pl.pallas_call(
        kernel,
        out_shape=out_shape,
        in_specs=in_specs,
        out_specs=out_specs,
        compiler_params=pltpu.CompilerParams(vmem_limit_bytes=mib * MIB),
        cost_estimate=pl.CostEstimate(flops=0, bytes_accessed=int(us * 3.0e6), transcendentals=0),
        name=name,
        **more,
    )(*args)


def groups_of(count):
    return lax.div(jnp.clip(count, 0, SLOTS) + (GROUP - 1), GROUP)


def fetch(vals_ref, vals, sems, count_ref, j, k):
    def each(action):
        @pl.loop(0, groups_of(count_ref[0, j]))
        def _(g):
            action(
                pltpu.make_async_copy(
                    vals_ref.at[pl.ds(pl.multiple_of(j * SLOTS + g * GROUP, GROUP), GROUP)],
                    vals.at[pl.ds(pl.multiple_of(k * SLOTS + g * GROUP, GROUP), GROUP)],
                    sems.at[k * GROUPS + g],
                )
            )

    return each


def add_list(panel, piece, vals, count_ref, lists_ref, j, k, wait=None):
    count = count_ref[0, j]

    @pl.loop(0, groups_of(count))
    def _(g):
        if wait is not None:
            wait(g)
        products, rows = [], []
        for u in range(GROUP):
            q = g * GROUP + u
            entry = jnp.where(q < count, lists_ref[j, q], PANEL_BLK * 4)
            rows.append(pl.ds(pl.multiple_of((entry >> 2) * BS, BS), BS))
            products.append(
                jnp.dot(
                    vals[k * SLOTS + q],
                    piece[pl.ds(pl.multiple_of((entry & 3) * BS, BS), BS), :],
                    preferred_element_type=jnp.float32,
                )
            )
        for row, product in zip(rows, products):
            panel[row, :] += product


def group_wait(vals_ref, vals, sems, j, k):
    def wait(g):
        pltpu.make_async_copy(
            vals_ref.at[pl.ds(pl.multiple_of(j * SLOTS + g * GROUP, GROUP), GROUP)],
            vals.at[pl.ds(pl.multiple_of(k * SLOTS + g * GROUP, GROUP), GROUP)],
            sems.at[k * GROUPS + g],
        ).wait()

    return wait


def piece_of(shift, flip):
    place = lax.axis_index("blk")
    x_hi = lax.rem(place, 2)
    return lax.rem(lax.div(place, 2) + shift, 4) * 2 + (1 - x_hi if flip else x_hi)


def first_products(count_ref, lists_ref, own_ref, vals_ref, panel, own, vals, sems, own_sem):
    mine = piece_of(0, False)
    own_copy = pltpu.make_async_copy(own_ref, own, own_sem)
    own_copy.start()
    fetch(vals_ref, vals, sems, count_ref, mine, 0)(lambda copy: copy.start())

    @pl.loop(0, PANEL_BLK // 4)
    def _(k):
        panel[pl.ds(pl.multiple_of(k * 4 * BS, 4 * BS), 4 * BS), :] = jnp.zeros((4 * BS, F), jnp.float32)

    own_copy.wait()
    add_list(panel, own, vals, count_ref, lists_ref, mine, 0, group_wait(vals_ref, vals, sems, mine, 0))


def more_products(pieces, ahead, count_ref, lists_ref, _, vals_ref, *refs):
    inputs = 1 + max(array for _, (array, _) in pieces)
    pairs, (panel, *outputs) = refs[:inputs], refs[inputs:]
    vals, sems = outputs[-2:]
    todo = [piece_of(*which) for which, _ in pieces]
    for k, j in enumerate(todo):
        fetch(vals_ref, vals, sems, count_ref, j, k)(lambda copy: copy.start())
    later = [
        fetch(vals_ref, outputs[0], outputs[1], count_ref, piece_of(*which), k)
        for k, which in enumerate(ahead)
    ]
    for each in later:
        each(lambda copy: copy.start())
    for k, (j, (_, (array, half))) in enumerate(zip(todo, pieces)):
        add_list(
            panel, pairs[array].at[half], vals, count_ref, lists_ref, j, k,
            group_wait(vals_ref, vals, sems, j, k),
        )
    for each in later:
        each(lambda copy: copy.wait())


def quantize(block):
    peak = jnp.maximum(jnp.max(jnp.abs(block), axis=0, keepdims=True), 1e-32)
    exponent = jnp.ceil(jnp.log2(peak) + 0.001)
    scaled = block * (jnp.exp2(-exponent) * TOP)
    return jnp.round(scaled).astype(jnp.int32).astype(jnp.int16), exponent


def write_message(out_ref, index, part, blocks):
    _, rows, count = part
    row = lax.broadcasted_iota(jnp.int32, (16, F), 0)
    tail = jnp.zeros((16, F), jnp.float32)
    for i, block in enumerate(blocks):
        whole, exponent = quantize(block)
        out_ref[index, i * rows : (i + 1) * rows, :] = whole
        tail = jnp.where(row == i, exponent, tail)
    out_ref[index, count * rows : count * rows + 16, :] = tail.astype(jnp.int32).astype(jnp.int16)


def read_message(ref, index, part):
    _, rows, count = part
    tail = ref[index, count * rows : count * rows + 16, :].astype(jnp.int32).astype(jnp.float32)
    size = jnp.exp2(tail) * (1.0 / TOP)
    blocks = []
    for i in range(count):
        whole = ref[index, i * rows : (i + 1) * rows, :].astype(jnp.int32).astype(jnp.float32)
        blocks.append(whole * size[i : i + 1, :])
    return blocks


def add(first, *others):
    for other in others:
        first = [a + b for a, b in zip(first, other)]
    return first


class Here:
    def __init__(self, panel=None):
        place = lax.axis_index("rep")
        self.core, self.x, self.z = lax.rem(place, 2), lax.div(place, 16), lax.rem(lax.div(place, 2), 8)
        self.panel = panel

    def z_of(self, shift):
        return lax.rem(self.z + shift + 8, 8)

    def partial(self, other_x, z, part, other_core=False):
        start, rows, count = part
        core = 1 - self.core if other_core else self.core
        owner = (1 - self.x if other_x else self.x) * 16 + z * 2 + core
        base = owner * PIECE_ROWS + start
        return [self.panel[pl.ds(pl.multiple_of(base + i * rows, 16), rows), :] for i in range(count)]


def for_each_z(unroll, action):
    @pl.loop(0, 8 // unroll)
    def _(k):
        for u in range(unroll):
            action(k * unroll + u)


def core_messages(part, other_x, panel, out_ref):
    here = Here(panel)
    for k, other in enumerate(other_x):
        for_each_z(
            4, lambda z: write_message(out_ref, k * 8 + z, part, here.partial(other, z, part, other_core=True))
        )


def last_products(pieces, count_ref, lists_ref, _, vals, *refs):
    *arrays, panel, out_ref = refs
    for k, (which, piece) in enumerate(zip(pieces, arrays)):
        add_list(panel, piece, vals, count_ref, lists_ref, piece_of(*which), k)
    core_messages(FIRST, (True,), panel, out_ref)


def pair_up(first_ref, second_ref, out_ref):
    out_ref[0] = first_ref[...]
    out_ref[1] = second_ref[...]


def x_messages(panel, rc_ref, out_ref):
    here = Here(panel)
    for_each_z(
        4, lambda z: write_message(out_ref, z, FIRST, add(here.partial(True, z, FIRST), read_message(rc_ref, z, FIRST)))
    )


def base_value(part, here, rc_ref, rx_ref, other, z):
    value = add(here.partial(other, z, part), read_message(rc_ref, other * 8 + z, part))
    return value if rx_ref is None else add(value, read_message(rx_ref, z, part))


def sides(part):
    return (0,) if part == FIRST else (0, 1)


def z_start(part, panel, rc_ref, rx_ref, down_ref, up_ref, two_ref, far_ref):
    here = Here(panel)
    for other in sides(part):
        for out_ref, index, shift in (
            (down_ref, 2 * other, -4), (down_ref, 2 * other + 1, -1), (up_ref, other, 2),
            (two_ref, other, -2), (far_ref, other, 3),
        ):
            write_message(out_ref, index, part, base_value(part, here, rc_ref, rx_ref, other, here.z_of(shift)))


def z_middle(part, panel, rc_ref, rx_ref, down_ref, up_ref, three_ref, one_ref):
    here = Here(panel)
    for other in sides(part):
        value = functools.partial(base_value, part, here, rc_ref, rx_ref, other)
        come = read_message(down_ref, 2 * other, part)
        write_message(three_ref, other, part, add(value(here.z_of(-3)), come))
        come = read_message(up_ref, other, part)
        write_message(one_ref, other, part, add(value(here.z_of(1)), come))


def arrivals(part, other, down_ref, *refs):
    return [read_message(down_ref, 2 * other + 1, part)] + [read_message(ref, other, part) for ref in refs]


def z_end(panel, rc_ref, *refs):
    here = Here(panel)
    *arrived, out_ref, sum_ref = refs
    value = base_value(SECOND, here, rc_ref, None, 1, here.z)
    write_message(out_ref, 0, SECOND, add(value, *arrivals(SECOND, 1, *arrived)))
    value = base_value(SECOND, here, rc_ref, None, 0, here.z)
    sum_ref[...] = add(value, *arrivals(SECOND, 0, *arrived))[0]


def layer(panel, rc_ref, rx_ref, sum_ref, rx2_ref, *refs):
    here = Here(panel)
    *arrived, weight_ref, out_ref = refs
    first = add(base_value(FIRST, here, rc_ref, rx_ref, 0, here.z), *arrivals(FIRST, 0, *arrived))
    second = add([sum_ref[...]], read_message(rx2_ref, 0, SECOND))
    weight = weight_ref[...]
    row = 0
    for block in first + second:
        high = block.astype(jnp.bfloat16)
        rest = block - high.astype(jnp.float32)
        middle = rest.astype(jnp.bfloat16)
        low = (rest - middle.astype(jnp.float32)).astype(jnp.bfloat16)
        result = jnp.dot(low, weight, preferred_element_type=jnp.float32)
        result += jnp.dot(middle, weight, preferred_element_type=jnp.float32)
        result += jnp.dot(high, weight, preferred_element_type=jnp.float32)
        out_ref[row : row + block.shape[0], :] = jnp.maximum(result, 0.0).astype(jnp.bfloat16)
        row += block.shape[0]


def messages(count, part):
    return jax.ShapeDtypeStruct((count, message_rows(part), F), jnp.int16)


def send_blk(array, dy, flip=0):
    pairs = [(y * 2 + h, ((y + dy) % 4) * 2 + (h ^ flip)) for y in range(4) for h in range(2)]
    return lax.ppermute(array, "blk", pairs)


def send_rep(array, dx, dz, dc):
    pairs = [
        (x * 16 + z * 2 + c, (x ^ dx) * 16 + ((z + dz) % 8) * 2 + (c ^ dc))
        for x in range(2) for z in range(8) for c in range(2)
    ]
    return lax.ppermute(array, "rep", pairs)


def sum_along_z(part, name, panel, rc, rx):
    count = len(sides(part))
    have = (rc,) if rx is None else (rc, rx)

    def fill(kernel):
        if rx is not None:
            return functools.partial(kernel, part)
        return lambda panel_ref, rc_ref, *refs: kernel(part, panel_ref, rc_ref, None, *refs)

    down, up, two, far = call(
        fill(z_start), name + "_start", (messages(2 * count, part),) + (messages(count, part),) * 3,
        [VMEM] * (1 + len(have)), (VMEM,) * 4, (panel, *have), 0.6,
    )
    down, up = send_rep(down, 0, -1, 0), send_rep(up, 0, 1, 0)
    two, far = send_rep(two, 0, -2, 0), send_rep(far, 0, 3, 0)
    three, one = call(
        fill(z_middle), name + "_middle", (messages(count, part),) * 2,
        [VMEM] * (3 + len(have)), (VMEM,) * 2, (panel, *have, down, up), 0.6,
    )
    return down, two, far, send_rep(three, 0, -3, 0), send_rep(one, 0, 1, 0)


def local(node_feats, block_vals, block_rows, block_cols, block_count, weight):
    slots = block_rows.reshape(LISTS, SLOTS) * 4 + block_cols.reshape(LISTS, SLOTS)
    lists = (block_count.reshape(1, LISTS), slots)
    vals = block_vals.reshape(LISTS * SLOTS, BS, BS)
    panel_type = jax.ShapeDtypeStruct(((PANEL_BLK + 1) * BS, F), jnp.float32)
    piece_buffer = pltpu.VMEM((PIECE_ROWS, F), jnp.bfloat16)

    def list_buffers(count):
        return [pltpu.VMEM((count * SLOTS, BS, BS), jnp.bfloat16), pltpu.SemaphoreType.DMA((count * GROUPS,))]

    own = node_feats
    flipped = send_blk(own, 0, 1)
    panel = call(
        first_products, "products_own", panel_type, [SMEM] * 2 + [ANY] * 2, VMEM, (*lists, own, vals), 3, 41,
        scratch_shapes=[piece_buffer, *list_buffers(1), pltpu.SemaphoreType.DMA],
    )
    panel, flipped = lax.optimization_barrier((panel, flipped))
    pair = call(
        pair_up, "pair", jax.ShapeDtypeStruct((2, PIECE_ROWS, F), jnp.bfloat16), [VMEM] * 2, VMEM, (own, flipped), 0.3
    )
    below, above = send_blk(pair, 1), send_blk(pair, -1)
    panel = call(
        functools.partial(more_products, (((0, True), (0, 1)),), ()), "products_flipped", panel_type,
        [SMEM] * 2 + [VMEM, ANY, VMEM], VMEM, (*lists, panel, vals, pair), 3, 41,
        input_output_aliases={2: 0},
        scratch_shapes=list_buffers(1),
    )
    panel, below, above = lax.optimization_barrier((panel, below, above))
    far = send_blk(below[0], 1), send_blk(above[1], -1)
    far_pieces = (2, False), (2, True)
    near_pieces = ((3, False), (0, 0)), ((3, True), (0, 1)), ((1, False), (1, 0)), ((1, True), (1, 1))
    panel, last_vals = call(
        functools.partial(more_products, near_pieces, far_pieces), "products_near",
        (panel_type, jax.ShapeDtypeStruct((2 * SLOTS, BS, BS), jnp.bfloat16)),
        [SMEM] * 2 + [VMEM, ANY] + [VMEM] * 2, (VMEM,) * 2, (*lists, panel, vals, below, above), 3, 41,
        input_output_aliases={2: 0},
        scratch_shapes=[pltpu.SemaphoreType.DMA((2 * GROUPS,)), *list_buffers(4)],
    )
    panel, to_core = call(
        functools.partial(last_products, far_pieces), "products_far", (panel_type, messages(8, FIRST)),
        [SMEM] * 2 + [VMEM] * 4, (VMEM,) * 2, (*lists, panel, last_vals, *far), 3, 40,
        input_output_aliases={2: 0},
    )

    def to_other_core(name, panel, part, other_x):
        return call(
            functools.partial(core_messages, part, other_x), name, messages(8 * len(other_x), part),
            [VMEM], VMEM, (panel,), 0.6,
        )

    rc_cross = send_rep(to_core, 0, 0, 1)
    rc_second = send_rep(to_other_core("core_second", panel, SECOND, (False, True)), 0, 0, 1)
    rc_first = send_rep(to_other_core("core_first", panel, FIRST, (False,)), 0, 0, 1)
    to_x = call(x_messages, "x_first", messages(8, FIRST), [VMEM, VMEM], VMEM, (panel, rc_cross), 0.6)
    rx_first = send_rep(to_x, 1, 0, 0)
    rc_second, rc_first = lax.optimization_barrier((rc_second, rc_first))
    second = sum_along_z(SECOND, "second", panel, rc_second, None)
    to_x, own_sum = call(
        z_end, "x_second", (messages(1, SECOND), jax.ShapeDtypeStruct((SECOND[1], F), jnp.float32)),
        [VMEM] * 7, (VMEM,) * 2, (panel, rc_second, *second), 0.6,
    )
    panel, to_x = lax.optimization_barrier((panel, to_x))
    rx_second = send_rep(to_x, 1, 0, 0)
    first = sum_along_z(FIRST, "first", panel, rc_first, rx_first)
    return call(
        layer, "layer", jax.ShapeDtypeStruct((PIECE_ROWS, H), jnp.bfloat16), [VMEM] * 11, VMEM,
        (panel, rc_first, rx_first, own_sum, rx_second, *first, weight), 1.5,
    )


def solution(mesh):
    return jax.shard_map(
        local,
        mesh=mesh,
        in_specs=(
            P(("blk", "rep"), None),
            P("blk", "rep", None, None, None, None),
            P("blk", "rep", None, None),
            P("blk", "rep", None, None),
            P("blk", "rep", None),
            P(),
        ),
        out_specs=P(("blk", "rep"), None),
        check_vma=False,
    )
```

```python
import functools

import jax
import jax.numpy as jnp
from jax import lax
from jax.experimental import pallas as pl
from jax.experimental.pallas import tpu as pltpu
from jax.sharding import PartitionSpec as P

BS = 128
F = 128
H = 256
SLOTS = 40
LISTS = 8
PIECE_BLK = 3
PIECE_ROWS = PIECE_BLK * BS
HALF = PIECE_ROWS // 2
PANEL_BLK = 96
GROUP = 8
GROUPS = SLOTS // GROUP
TOP = 32766.0
MIB = 1 << 20

FIRST, SECOND = (0, 144, 2), (288, 96, 1)


SMEM = pl.BlockSpec(memory_space=pltpu.SMEM)
VMEM = pl.BlockSpec(memory_space=pltpu.VMEM)
ANY = pl.BlockSpec(memory_space=pl.ANY)


def call(kernel, name, out_shape, in_specs, out_specs, args, us, mib=24, **more):
    return pl.pallas_call(
        kernel,
        out_shape=out_shape,
        in_specs=in_specs,
        out_specs=out_specs,
        compiler_params=pltpu.CompilerParams(vmem_limit_bytes=mib * MIB),
        cost_estimate=pl.CostEstimate(flops=0, bytes_accessed=int(us * 3.0e6), transcendentals=0),
        name=name,
        **more,
    )(*args)


def groups_of(count):
    return lax.div(jnp.clip(count, 0, SLOTS) + (GROUP - 1), GROUP)


def fetch(vals_ref, vals, sems, lists_ref, j, k):
    def each(action):
        @pl.loop(0, groups_of(lists_ref[j, 0] & 63))
        def _(g):
            action(
                pltpu.make_async_copy(
                    vals_ref.at[pl.ds(pl.multiple_of(j * SLOTS + g * GROUP, GROUP), GROUP)],
                    vals.at[pl.ds(pl.multiple_of(k * SLOTS + g * GROUP, GROUP), GROUP)],
                    sems.at[k * GROUPS + g],
                )
            )

    return each


def add_list(panel, piece, vals, lists_ref, j, k, wait=None):
    count = lists_ref[j, 0] & 63

    @pl.loop(0, groups_of(count))
    def _(g):
        if wait is not None:
            wait(g)
        products, rows = [], []
        for u in range(GROUP):
            q = g * GROUP + u
            entry = jnp.where(q < count, lists_ref[j, q] >> 6, PANEL_BLK * 4)
            rows.append(pl.ds(pl.multiple_of((entry >> 2) * BS, BS), BS))
            products.append(
                jnp.dot(
                    vals[k * SLOTS + q],
                    piece[pl.ds(pl.multiple_of((entry & 3) * BS, BS), BS), :],
                    preferred_element_type=jnp.float32,
                )
            )
        for row, product in zip(rows, products):
            panel[row, :] += product


def group_wait(vals_ref, vals, sems, j, k):
    def wait(g):
        pltpu.make_async_copy(
            vals_ref.at[pl.ds(pl.multiple_of(j * SLOTS + g * GROUP, GROUP), GROUP)],
            vals.at[pl.ds(pl.multiple_of(k * SLOTS + g * GROUP, GROUP), GROUP)],
            sems.at[k * GROUPS + g],
        ).wait()

    return wait


def piece_of(shift, flip):
    place = lax.axis_index("blk")
    x_hi = lax.rem(place, 2)
    return lax.rem(lax.div(place, 2) + shift, 4) * 2 + (1 - x_hi if flip else x_hi)


def hold(own_ref, out_ref):
    out_ref[...] = own_ref[...]


def first_products(which, ahead, lists_ref, own_ref, flipped_ref, vals_ref, panel, next_vals, *scratch):
    vals, sems, next_sems = scratch
    todo = [piece_of(*piece) for piece in which]
    for k, j in enumerate(todo):
        fetch(vals_ref, vals, sems, lists_ref, j, k)(lambda copy: copy.start())
    later = [
        fetch(vals_ref, next_vals, next_sems, lists_ref, piece_of(*piece), k) for k, piece in enumerate(ahead)
    ]
    for each in later:
        each(lambda copy: copy.start())

    @pl.loop(0, PANEL_BLK // 4)
    def _(k):
        panel[pl.ds(pl.multiple_of(k * 4 * BS, 4 * BS), 4 * BS), :] = jnp.zeros((4 * BS, F), jnp.float32)

    for k, (j, piece) in enumerate(zip(todo, (own_ref, flipped_ref))):
        add_list(panel, piece, vals, lists_ref, j, k, group_wait(vals_ref, vals, sems, j, k))
    for each in later:
        each(lambda copy: copy.wait())


def more_products(pieces, first, lists_ref, _, vals, *refs):
    *arrays, panel = refs
    for k, (piece, array) in enumerate(zip(pieces, arrays)):
        add_list(panel, array, vals, lists_ref, piece_of(*piece), first + k)


def quantize(block):
    peak = jnp.maximum(jnp.max(jnp.abs(block), axis=0, keepdims=True), 1e-32)
    exponent = jnp.ceil(jnp.log2(peak) + 0.001)
    scaled = block * (jnp.exp2(-exponent) * TOP)
    return jnp.round(scaled).astype(jnp.int32).astype(jnp.int16), exponent


def messages(count, part):
    return jax.ShapeDtypeStruct((count * part[1] * part[2] + 16, F), jnp.int16)


def write_messages(out_ref, part, values):
    _, rows, count = part
    row = lax.broadcasted_iota(jnp.int32, (16, F), 0)
    tail = jnp.zeros((16, F), jnp.float32)
    k = 0
    for value in values:
        for block in value():
            whole, exponent = quantize(block)
            out_ref[k * rows : (k + 1) * rows, :] = whole
            tail = jnp.where(row == k, exponent, tail)
            k += 1
    out_ref[k * rows : k * rows + 16, :] = tail.astype(jnp.int32).astype(jnp.int16)


def read_message(ref, index, part):
    _, rows, count = part
    last = ref.shape[0] - 16
    row = lax.broadcasted_iota(jnp.int32, (16, F), 0)
    tail = ref[last : last + 16, :].astype(jnp.int32).astype(jnp.float32)
    blocks = []
    for i in range(count):
        k = index * count + i
        if isinstance(k, int):
            exponent = tail[k : k + 1, :]
            whole = ref[k * rows : (k + 1) * rows, :]
        else:
            exponent = jnp.sum(jnp.where(row == k, tail, 0.0), axis=0, keepdims=True)
            whole = ref[pl.ds(pl.multiple_of(k * rows, 16), rows), :]
        blocks.append(whole.astype(jnp.int32).astype(jnp.float32) * (jnp.exp2(exponent) * (1.0 / TOP)))
    return blocks


def add(first, *others):
    for other in others:
        first = [a + b for a, b in zip(first, other)]
    return first


class Here:
    def __init__(self, panel=None):
        place = lax.axis_index("rep")
        self.core, self.x, self.z = lax.rem(place, 2), lax.div(place, 16), lax.rem(lax.div(place, 2), 8)
        self.panel = panel

    def z_of(self, shift):
        return lax.rem(self.z + shift + 8, 8)

    def partial(self, other_x, z, part, other_core=False):
        start, rows, count = part
        core = 1 - self.core if other_core else self.core
        owner = (1 - self.x if other_x else self.x) * 16 + z * 2 + core
        base = owner * PIECE_ROWS + start
        return [self.panel[pl.ds(pl.multiple_of(base + i * rows, 16), rows), :] for i in range(count)]


def core_messages(part, other_x, panel, out_ref):
    here = Here(panel)
    write_messages(
        out_ref, part,
        [
            functools.partial(here.partial, other, z, part, other_core=True)
            for other in other_x for z in range(8)
        ],
    )


def last_products(pieces, first, *refs):
    more_products(pieces, first, *refs[:-1])
    core_messages(FIRST, (True,), *refs[-2:])


def x_messages(panel, rc_ref, out_ref):
    here = Here(panel)
    write_messages(
        out_ref, FIRST,
        [lambda z=z: add(here.partial(True, z, FIRST), read_message(rc_ref, z, FIRST)) for z in range(8)],
    )


def base_value(part, here, rc_ref, rx_ref, other, z):
    value = add(here.partial(other, z, part), read_message(rc_ref, other * 8 + z, part))
    return value if rx_ref is None else add(value, read_message(rx_ref, z, part))


def sides(part):
    return (0,) if part == FIRST else (0, 1)


def z_start(part, panel, rc_ref, rx_ref, down_ref, up_ref, two_ref, far_ref):
    here = Here(panel)
    for out_ref, shifts in ((down_ref, (-4, -1)), (up_ref, (2,)), (two_ref, (-2,)), (far_ref, (3,))):
        write_messages(
            out_ref, part,
            [
                functools.partial(base_value, part, here, rc_ref, rx_ref, other, here.z_of(shift))
                for other in sides(part) for shift in shifts
            ],
        )


def z_middle(part, panel, rc_ref, rx_ref, down_ref, up_ref, three_ref, one_ref):
    here = Here(panel)

    def through(come_ref, stride, shift):
        return [
            lambda other=other: add(
                base_value(part, here, rc_ref, rx_ref, other, here.z_of(shift)),
                read_message(come_ref, stride * other, part),
            )
            for other in sides(part)
        ]

    write_messages(three_ref, part, through(down_ref, 2, -3))
    write_messages(one_ref, part, through(up_ref, 1, 1))


def arrivals(part, other, down_ref, *refs):
    return [read_message(down_ref, 2 * other + 1, part)] + [read_message(ref, other, part) for ref in refs]


def z_end(panel, rc_ref, *refs):
    here = Here(panel)
    *arrived, out_ref, sum_ref = refs
    value = base_value(SECOND, here, rc_ref, None, 1, here.z)
    write_messages(out_ref, SECOND, [lambda: add(value, *arrivals(SECOND, 1, *arrived))])
    mine = base_value(SECOND, here, rc_ref, None, 0, here.z)
    sum_ref[...] = add(mine, *arrivals(SECOND, 0, *arrived))[0]


def layer(panel, rc_ref, rx_ref, sum_ref, rx2_ref, *refs):
    here = Here(panel)
    *arrived, weight_ref, out_ref = refs
    first = add(base_value(FIRST, here, rc_ref, rx_ref, 0, here.z), *arrivals(FIRST, 0, *arrived))
    second = add([sum_ref[...]], read_message(rx2_ref, 0, SECOND))
    weight = weight_ref[...]
    row = 0
    for block in first + second:
        high = block.astype(jnp.bfloat16)
        rest = block - high.astype(jnp.float32)
        middle = rest.astype(jnp.bfloat16)
        low = (rest - middle.astype(jnp.float32)).astype(jnp.bfloat16)
        result = jnp.dot(low, weight, preferred_element_type=jnp.float32)
        result += jnp.dot(middle, weight, preferred_element_type=jnp.float32)
        result += jnp.dot(high, weight, preferred_element_type=jnp.float32)
        out_ref[row : row + block.shape[0], :] = jnp.maximum(result, 0.0).astype(jnp.bfloat16)
        row += block.shape[0]


def send_blk(array, dy, flip=0):
    pairs = [(y * 2 + h, ((y + dy) % 4) * 2 + (h ^ flip)) for y in range(4) for h in range(2)]
    return lax.ppermute(array, "blk", pairs)


def send_rep(array, dx, dz, dc):
    pairs = [
        (x * 16 + z * 2 + c, (x ^ dx) * 16 + ((z + dz) % 8) * 2 + (c ^ dc))
        for x in range(2) for z in range(8) for c in range(2)
    ]
    return lax.ppermute(array, "rep", pairs)


def sum_along_z(part, name, panel, rc, rx):
    count = len(sides(part))
    have = (rc,) if rx is None else (rc, rx)

    def fill(kernel):
        if rx is not None:
            return functools.partial(kernel, part)
        return lambda panel_ref, rc_ref, *refs: kernel(part, panel_ref, rc_ref, None, *refs)

    down, up, two, far = call(
        fill(z_start), name + "_start", (messages(2 * count, part),) + (messages(count, part),) * 3,
        [VMEM] * (1 + len(have)), (VMEM,) * 4, (panel, *have), 0.6,
    )
    down, up = send_rep(down, 0, -1, 0), send_rep(up, 0, 1, 0)
    two, far = send_rep(two, 0, -2, 0), send_rep(far, 0, 3, 0)
    three, one = call(
        fill(z_middle), name + "_middle", (messages(count, part),) * 2,
        [VMEM] * (3 + len(have)), (VMEM,) * 2, (panel, *have, down, up), 0.6,
    )
    return down, two, far, send_rep(three, 0, -3, 0), send_rep(one, 0, 1, 0)


def local(node_feats, block_vals, block_rows, block_cols, block_count, weight):
    vals = block_vals.reshape(LISTS * SLOTS, BS, BS)
    panel_type = jax.ShapeDtypeStruct(((PANEL_BLK + 1) * BS, F), jnp.float32)
    here, near, far = ((0, False), (0, True)), ((3, False), (1, False), (3, True), (1, True)), ((2, False), (2, True))
    own = node_feats
    flipped, below, above = send_blk(own, 0, 1), send_blk(own, 1), send_blk(own, -1)
    own = call(hold, "own_piece", jax.ShapeDtypeStruct((PIECE_ROWS, F), jnp.bfloat16), [VMEM], VMEM, (own,), 1)
    slots = block_rows.reshape(LISTS, SLOTS) * 4 + block_cols.reshape(LISTS, SLOTS)
    lists = slots * 64 + block_count.reshape(LISTS, 1)
    flipped, own, lists = lax.optimization_barrier((flipped, own, lists))
    below_flipped, above_flipped = send_blk(flipped, 1), send_blk(flipped, -1)
    later = len(near) + len(far)
    panel, next_vals = call(
        functools.partial(first_products, here, near + far), "products_here",
        (panel_type, jax.ShapeDtypeStruct((later * SLOTS, BS, BS), jnp.bfloat16)),
        [SMEM, VMEM, VMEM, ANY], (VMEM,) * 2, (lists, own, flipped, vals), 4, 40,
        scratch_shapes=[
            pltpu.VMEM((2 * SLOTS, BS, BS), jnp.bfloat16),
            pltpu.SemaphoreType.DMA((2 * GROUPS,)),
            pltpu.SemaphoreType.DMA((later * GROUPS,)),
        ],
    )
    panel, below, above, below_flipped, above_flipped = lax.optimization_barrier(
        (panel, below, above, below_flipped, above_flipped)
    )
    far_own, far_flipped = send_blk(below, 1), send_blk(above_flipped, -1)
    panel = call(
        functools.partial(more_products, near, 0), "products_near", panel_type,
        [SMEM] + [VMEM] * 6, VMEM,
        (lists, panel, next_vals, below, above, below_flipped, above_flipped), 3, 24,
        input_output_aliases={1: 0},
    )
    panel, to_core = call(
        functools.partial(last_products, far, len(near)), "products_far", (panel_type, messages(8, FIRST)),
        [SMEM] + [VMEM] * 4, (VMEM,) * 2, (lists, panel, next_vals, far_own, far_flipped), 3, 24,
        input_output_aliases={1: 0},
    )

    def to_other_core(name, panel, part, other_x):
        return call(
            functools.partial(core_messages, part, other_x), name, messages(8 * len(other_x), part),
            [VMEM], VMEM, (panel,), 0.6,
        )

    rc_cross = send_rep(to_core, 0, 0, 1)
    rc_second = send_rep(to_other_core("core_second", panel, SECOND, (False, True)), 0, 0, 1)
    rc_first = send_rep(to_other_core("core_first", panel, FIRST, (False,)), 0, 0, 1)
    rc_cross, rc_second = lax.optimization_barrier((rc_cross, rc_second))
    to_x = call(x_messages, "x_first", messages(8, FIRST), [VMEM, VMEM], VMEM, (panel, rc_cross), 0.6)
    rx_first = send_rep(to_x, 1, 0, 0)
    rc_second, rc_first = lax.optimization_barrier((rc_second, rc_first))
    second = sum_along_z(SECOND, "second", panel, rc_second, None)
    to_x, own_sum = call(
        z_end, "x_second", (messages(1, SECOND), jax.ShapeDtypeStruct((SECOND[1], F), jnp.float32)),
        [VMEM] * 7, (VMEM,) * 2, (panel, rc_second, *second), 0.6,
    )
    panel, to_x = lax.optimization_barrier((panel, to_x))
    rx_second = send_rep(to_x, 1, 0, 0)
    first = sum_along_z(FIRST, "first", panel, rc_first, rx_first)
    return call(
        layer, "layer", jax.ShapeDtypeStruct((PIECE_ROWS, H), jnp.bfloat16), [VMEM] * 11, VMEM,
        (panel, rc_first, rx_first, own_sum, rx_second, *first, weight), 1.5,
    )


def solution(mesh):
    return jax.shard_map(
        local,
        mesh=mesh,
        in_specs=(
            P(("blk", "rep"), None),
            P("blk", "rep", None, None, None, None),
            P("blk", "rep", None, None),
            P("blk", "rep", None, None),
            P("blk", "rep", None),
            P(),
        ),
        out_specs=P(("blk", "rep"), None),
        check_vma=False,
    )
```

```python
import functools

import jax
import jax.numpy as jnp
from jax import lax
from jax.experimental import pallas as pl
from jax.experimental.pallas import tpu as pltpu
from jax.sharding import PartitionSpec as P

BS = 128
F = 128
H = 256
SLOTS = 40
LISTS = 8
PIECE_BLK = 3
PIECE_ROWS = PIECE_BLK * BS
HALF = PIECE_ROWS // 2
PANEL_BLK = 96
GROUP = 8
GROUPS = SLOTS // GROUP
TOP = 32766.0
MIB = 1 << 20

FIRST, SECOND = (0, 144, 2), (288, 96, 1)


SMEM = pl.BlockSpec(memory_space=pltpu.SMEM)
VMEM = pl.BlockSpec(memory_space=pltpu.VMEM)
ANY = pl.BlockSpec(memory_space=pl.ANY)


def call(kernel, name, out_shape, in_specs, out_specs, args, us, mib=24, **more):
    return pl.pallas_call(
        kernel,
        out_shape=out_shape,
        in_specs=in_specs,
        out_specs=out_specs,
        compiler_params=pltpu.CompilerParams(vmem_limit_bytes=mib * MIB),
        cost_estimate=pl.CostEstimate(flops=0, bytes_accessed=int(us * 3.0e6), transcendentals=0),
        name=name,
        **more,
    )(*args)


def groups_of(count):
    return lax.div(jnp.clip(count, 0, SLOTS) + (GROUP - 1), GROUP)


def fetch(vals_ref, vals, sems, lists_ref, j, k):
    def each(action):
        @pl.loop(0, groups_of(lists_ref[j, 0] & 63))
        def _(g):
            action(
                pltpu.make_async_copy(
                    vals_ref.at[pl.ds(pl.multiple_of(j * SLOTS + g * GROUP, GROUP), GROUP)],
                    vals.at[pl.ds(pl.multiple_of(k * SLOTS + g * GROUP, GROUP), GROUP)],
                    sems.at[k * GROUPS + g],
                )
            )

    return each


def add_list(panel, piece, vals, lists_ref, j, k, wait=None):
    count = lists_ref[j, 0] & 63

    @pl.loop(0, groups_of(count))
    def _(g):
        if wait is not None:
            wait(g)
        products, rows = [], []
        for u in range(GROUP):
            q = g * GROUP + u
            entry = jnp.where(q < count, lists_ref[j, q] >> 6, PANEL_BLK * 4)
            rows.append(pl.ds(pl.multiple_of((entry >> 2) * BS, BS), BS))
            products.append(
                jnp.dot(
                    vals[k * SLOTS + q],
                    piece[pl.ds(pl.multiple_of((entry & 3) * BS, BS), BS), :],
                    preferred_element_type=jnp.float32,
                )
            )
        for row, product in zip(rows, products):
            panel[row, :] += product


def group_wait(vals_ref, vals, sems, j, k):
    def wait(g):
        pltpu.make_async_copy(
            vals_ref.at[pl.ds(pl.multiple_of(j * SLOTS + g * GROUP, GROUP), GROUP)],
            vals.at[pl.ds(pl.multiple_of(k * SLOTS + g * GROUP, GROUP), GROUP)],
            sems.at[k * GROUPS + g],
        ).wait()

    return wait


def piece_of(shift, flip):
    place = lax.axis_index("blk")
    x_hi = lax.rem(place, 2)
    return lax.rem(lax.div(place, 2) + shift, 4) * 2 + (1 - x_hi if flip else x_hi)


def hold(own_ref, out_ref):
    out_ref[...] = own_ref[...]


def first_products(which, ahead, lists_ref, own_ref, flipped_ref, vals_ref, panel, next_vals, *scratch):
    vals, sems, next_sems = scratch
    todo = [piece_of(*piece) for piece in which]
    for k, j in enumerate(todo):
        fetch(vals_ref, vals, sems, lists_ref, j, k)(lambda copy: copy.start())
    later = [
        fetch(vals_ref, next_vals, next_sems, lists_ref, piece_of(*piece), k) for k, piece in enumerate(ahead)
    ]
    for each in later:
        each(lambda copy: copy.start())

    @pl.loop(0, PANEL_BLK // 4)
    def _(k):
        panel[pl.ds(pl.multiple_of(k * 4 * BS, 4 * BS), 4 * BS), :] = jnp.zeros((4 * BS, F), jnp.float32)

    for k, (j, piece) in enumerate(zip(todo, (own_ref, flipped_ref))):
        add_list(panel, piece, vals, lists_ref, j, k, group_wait(vals_ref, vals, sems, j, k))
    for each in later:
        each(lambda copy: copy.wait())


def more_products(pieces, first, lists_ref, _, vals, *refs):
    *arrays, panel = refs
    for k, (piece, array) in enumerate(zip(pieces, arrays)):
        add_list(panel, array, vals, lists_ref, piece_of(*piece), first + k)


def quantize(block):
    peak = jnp.maximum(jnp.max(jnp.abs(block), axis=0, keepdims=True), 1e-32)
    exponent = jnp.ceil(jnp.log2(peak) + 0.001)
    scaled = block * (jnp.exp2(-exponent) * TOP)
    return jnp.round(scaled).astype(jnp.int32).astype(jnp.int16), exponent


def messages(count, part):
    return jax.ShapeDtypeStruct((count * part[1] * part[2] + 16, F), jnp.int16)


def write_messages(out_ref, part, values):
    _, rows, count = part
    row = lax.broadcasted_iota(jnp.int32, (16, F), 0)
    tail = jnp.zeros((16, F), jnp.float32)
    k = 0
    for value in values:
        for block in value():
            whole, exponent = quantize(block)
            out_ref[k * rows : (k + 1) * rows, :] = whole
            tail = jnp.where(row == k, exponent, tail)
            k += 1
    out_ref[k * rows : k * rows + 16, :] = tail.astype(jnp.int32).astype(jnp.int16)


def read_message(ref, index, part):
    _, rows, count = part
    last = ref.shape[0] - 16
    row = lax.broadcasted_iota(jnp.int32, (16, F), 0)
    tail = ref[last : last + 16, :].astype(jnp.int32).astype(jnp.float32)
    blocks = []
    for i in range(count):
        k = index * count + i
        if isinstance(k, int):
            exponent = tail[k : k + 1, :]
            whole = ref[k * rows : (k + 1) * rows, :]
        else:
            exponent = jnp.sum(jnp.where(row == k, tail, 0.0), axis=0, keepdims=True)
            whole = ref[pl.ds(pl.multiple_of(k * rows, 16), rows), :]
        blocks.append(whole.astype(jnp.int32).astype(jnp.float32) * (jnp.exp2(exponent) * (1.0 / TOP)))
    return blocks


def add(first, *others):
    for other in others:
        first = [a + b for a, b in zip(first, other)]
    return first


class Here:
    def __init__(self, panel=None):
        place = lax.axis_index("rep")
        self.core, self.x, self.z = lax.rem(place, 2), lax.div(place, 16), lax.rem(lax.div(place, 2), 8)
        self.panel = panel

    def z_of(self, shift):
        return lax.rem(self.z + shift + 8, 8)

    def partial(self, other_x, z, part, other_core=False):
        start, rows, count = part
        core = 1 - self.core if other_core else self.core
        owner = (1 - self.x if other_x else self.x) * 16 + z * 2 + core
        base = owner * PIECE_ROWS + start
        return [self.panel[pl.ds(pl.multiple_of(base + i * rows, 16), rows), :] for i in range(count)]


def core_messages(part, other_x, panel, out_ref):
    here = Here(panel)
    write_messages(
        out_ref, part,
        [
            functools.partial(here.partial, other, z, part, other_core=True)
            for other in other_x for z in range(8)
        ],
    )


def last_products(pieces, first, *refs):
    more_products(pieces, first, *refs[:-1])
    core_messages(FIRST, (True,), *refs[-2:])


def rest_to_core(panel, out_ref):
    core_messages(SECOND, (False, True), panel, core_part(out_ref, SECOND))
    core_messages(FIRST, (False,), panel, core_part(out_ref, FIRST))


def core_part(ref, part):
    second_rows, first_rows = messages(16, SECOND).shape[0], messages(8, FIRST).shape[0]
    return ref.at[pl.ds(0, second_rows)] if part == SECOND else ref.at[pl.ds(second_rows, first_rows)]


def x_messages(panel, rc_ref, out_ref):
    here = Here(panel)
    write_messages(
        out_ref, FIRST,
        [lambda z=z: add(here.partial(True, z, FIRST), read_message(rc_ref, z, FIRST)) for z in range(8)],
    )


def base_value(part, here, rc_ref, rx_ref, other, z):
    value = add(here.partial(other, z, part), read_message(core_part(rc_ref, part), other * 8 + z, part))
    return value if rx_ref is None else add(value, read_message(rx_ref, z, part))


def sides(part):
    return (0,) if part == FIRST else (0, 1)


def z_start(part, panel, rc_ref, rx_ref, down_ref, up_ref, two_ref, far_ref):
    here = Here(panel)
    for out_ref, shifts in ((down_ref, (-4, -1)), (up_ref, (2,)), (two_ref, (-2,)), (far_ref, (3,))):
        write_messages(
            out_ref, part,
            [
                functools.partial(base_value, part, here, rc_ref, rx_ref, other, here.z_of(shift))
                for other in sides(part) for shift in shifts
            ],
        )


def z_middle(part, panel, rc_ref, rx_ref, down_ref, up_ref, three_ref, one_ref):
    here = Here(panel)

    def through(come_ref, stride, shift):
        return [
            lambda other=other: add(
                base_value(part, here, rc_ref, rx_ref, other, here.z_of(shift)),
                read_message(come_ref, stride * other, part),
            )
            for other in sides(part)
        ]

    write_messages(three_ref, part, through(down_ref, 2, -3))
    write_messages(one_ref, part, through(up_ref, 1, 1))


def arrivals(part, other, down_ref, *refs):
    return [read_message(down_ref, 2 * other + 1, part)] + [read_message(ref, other, part) for ref in refs]


def z_end(panel, rc_ref, *refs):
    here = Here(panel)
    *arrived, out_ref, sum_ref = refs
    value = base_value(SECOND, here, rc_ref, None, 1, here.z)
    write_messages(out_ref, SECOND, [lambda: add(value, *arrivals(SECOND, 1, *arrived))])
    mine = base_value(SECOND, here, rc_ref, None, 0, here.z)
    sum_ref[...] = add(mine, *arrivals(SECOND, 0, *arrived))[0]


def layer(panel, rc_ref, rx_ref, sum_ref, rx2_ref, *refs):
    here = Here(panel)
    *arrived, weight_ref, out_ref = refs
    first = add(base_value(FIRST, here, rc_ref, rx_ref, 0, here.z), *arrivals(FIRST, 0, *arrived))
    second = add([sum_ref[...]], read_message(rx2_ref, 0, SECOND))
    weight = weight_ref[...]
    row = 0
    for block in first + second:
        high = block.astype(jnp.bfloat16)
        rest = block - high.astype(jnp.float32)
        middle = rest.astype(jnp.bfloat16)
        low = (rest - middle.astype(jnp.float32)).astype(jnp.bfloat16)
        result = jnp.dot(low, weight, preferred_element_type=jnp.float32)
        result += jnp.dot(middle, weight, preferred_element_type=jnp.float32)
        result += jnp.dot(high, weight, preferred_element_type=jnp.float32)
        out_ref[row : row + block.shape[0], :] = jnp.maximum(result, 0.0).astype(jnp.bfloat16)
        row += block.shape[0]


def send_blk(array, dy, flip=0):
    pairs = [(y * 2 + h, ((y + dy) % 4) * 2 + (h ^ flip)) for y in range(4) for h in range(2)]
    return lax.ppermute(array, "blk", pairs)


def send_rep(array, dx, dz, dc):
    pairs = [
        (x * 16 + z * 2 + c, (x ^ dx) * 16 + ((z + dz) % 8) * 2 + (c ^ dc))
        for x in range(2) for z in range(8) for c in range(2)
    ]
    return lax.ppermute(array, "rep", pairs)


def sum_along_z(part, name, panel, rc, rx):
    count = len(sides(part))
    have = (rc,) if rx is None else (rc, rx)

    def fill(kernel):
        if rx is not None:
            return functools.partial(kernel, part)
        return lambda panel_ref, rc_ref, *refs: kernel(part, panel_ref, rc_ref, None, *refs)

    down, up, two, far = call(
        fill(z_start), name + "_start", (messages(2 * count, part),) + (messages(count, part),) * 3,
        [VMEM] * (1 + len(have)), (VMEM,) * 4, (panel, *have), 0.6,
    )
    down, up = send_rep(down, 0, -1, 0), send_rep(up, 0, 1, 0)
    two, far = send_rep(two, 0, -2, 0), send_rep(far, 0, 3, 0)
    three, one = call(
        fill(z_middle), name + "_middle", (messages(count, part),) * 2,
        [VMEM] * (3 + len(have)), (VMEM,) * 2, (panel, *have, down, up), 0.6,
    )
    return down, two, far, send_rep(three, 0, -3, 0), send_rep(one, 0, 1, 0)


def local(node_feats, block_vals, block_rows, block_cols, block_count, weight):
    vals = block_vals.reshape(LISTS * SLOTS, BS, BS)
    panel_type = jax.ShapeDtypeStruct(((PANEL_BLK + 1) * BS, F), jnp.float32)
    here, near, far = ((0, False), (0, True)), ((3, False), (1, False), (3, True), (1, True), (2, False)), ((2, True),)
    own = node_feats
    flipped, below, above = send_blk(own, 0, 1), send_blk(own, 1), send_blk(own, -1)
    own = call(hold, "own_piece", jax.ShapeDtypeStruct((PIECE_ROWS, F), jnp.bfloat16), [VMEM], VMEM, (own,), 1)
    slots = block_rows.reshape(LISTS, SLOTS) * 4 + block_cols.reshape(LISTS, SLOTS)
    lists = slots * 64 + block_count.reshape(LISTS, 1)
    flipped, own, lists = lax.optimization_barrier((flipped, own, lists))
    below_flipped, above_flipped, far_own = send_blk(flipped, 1), send_blk(flipped, -1), send_blk(below, 1)
    later = len(near) + len(far)
    panel, next_vals = call(
        functools.partial(first_products, here, near + far), "products_here",
        (panel_type, jax.ShapeDtypeStruct((later * SLOTS, BS, BS), jnp.bfloat16)),
        [SMEM, VMEM, VMEM, ANY], (VMEM,) * 2, (lists, own, flipped, vals), 4, 40,
        scratch_shapes=[
            pltpu.VMEM((2 * SLOTS, BS, BS), jnp.bfloat16),
            pltpu.SemaphoreType.DMA((2 * GROUPS,)),
            pltpu.SemaphoreType.DMA((later * GROUPS,)),
        ],
    )
    panel, above, below_flipped, above_flipped, far_own = lax.optimization_barrier(
        (panel, above, below_flipped, above_flipped, far_own)
    )
    far_flipped = send_blk(above_flipped, -1)
    panel = call(
        functools.partial(more_products, near, 0), "products_near", panel_type,
        [SMEM] + [VMEM] * 7, VMEM,
        (lists, panel, next_vals, below, above, below_flipped, above_flipped, far_own), 3, 24,
        input_output_aliases={1: 0},
    )
    panel, to_core = call(
        functools.partial(last_products, far, len(near)), "products_far", (panel_type, messages(8, FIRST)),
        [SMEM] + [VMEM] * 3, (VMEM,) * 2, (lists, panel, next_vals, far_flipped), 3, 24,
        input_output_aliases={1: 0},
    )

    rc_cross = send_rep(to_core, 0, 0, 1)
    second_rows, first_rows = messages(16, SECOND).shape[0], messages(8, FIRST).shape[0]
    to_core = call(
        rest_to_core, "core_rest", jax.ShapeDtypeStruct((second_rows + first_rows, F), jnp.int16),
        [VMEM], VMEM, (panel,), 0.3,
    )
    rc = send_rep(to_core, 0, 0, 1)
    to_x = call(x_messages, "x_first", messages(8, FIRST), [VMEM, VMEM], VMEM, (panel, rc_cross), 0.6)
    rx_first = send_rep(to_x, 1, 0, 0)
    second = sum_along_z(SECOND, "second", panel, rc, None)
    to_x, own_sum = call(
        z_end, "x_second", (messages(1, SECOND), jax.ShapeDtypeStruct((SECOND[1], F), jnp.float32)),
        [VMEM] * 7, (VMEM,) * 2, (panel, rc, *second), 0.6,
    )
    panel, to_x = lax.optimization_barrier((panel, to_x))
    rx_second = send_rep(to_x, 1, 0, 0)
    first = sum_along_z(FIRST, "first", panel, rc, rx_first)
    return call(
        layer, "layer", jax.ShapeDtypeStruct((PIECE_ROWS, H), jnp.bfloat16), [VMEM] * 11, VMEM,
        (panel, rc, rx_first, own_sum, rx_second, *first, weight), 1.5,
    )


def solution(mesh):
    return jax.shard_map(
        local,
        mesh=mesh,
        in_specs=(
            P(("blk", "rep"), None),
            P("blk", "rep", None, None, None, None),
            P("blk", "rep", None, None),
            P("blk", "rep", None, None),
            P("blk", "rep", None),
            P(),
        ),
        out_specs=P(("blk", "rep"), None),
        check_vma=False,
    )
```

```python
import functools

import jax
import jax.numpy as jnp
from jax import lax
from jax.experimental import pallas as pl
from jax.experimental.pallas import tpu as pltpu
from jax.sharding import PartitionSpec as P

BS = 128
F = 128
H = 256
SLOTS = 40
LISTS = 8
PIECE_BLK = 3
PIECE_ROWS = PIECE_BLK * BS
HALF = PIECE_ROWS // 2
PANEL_BLK = 96
GROUP = 8
GROUPS = SLOTS // GROUP
TOP = 32766.0
MIB = 1 << 20

FIRST, SECOND = (0, 144, 2), (288, 96, 1)


SMEM = pl.BlockSpec(memory_space=pltpu.SMEM)
VMEM = pl.BlockSpec(memory_space=pltpu.VMEM)
ANY = pl.BlockSpec(memory_space=pl.ANY)


def call(kernel, name, out_shape, in_specs, out_specs, args, us, mib=24, **more):
    return pl.pallas_call(
        kernel,
        out_shape=out_shape,
        in_specs=in_specs,
        out_specs=out_specs,
        compiler_params=pltpu.CompilerParams(vmem_limit_bytes=mib * MIB),
        cost_estimate=pl.CostEstimate(flops=0, bytes_accessed=int(us * 3.0e6), transcendentals=0),
        name=name,
        **more,
    )(*args)


def groups_of(count):
    return lax.div(jnp.clip(count, 0, SLOTS) + (GROUP - 1), GROUP)


def fetch(vals_ref, vals, sems, lists_ref, j, k):
    def each(action):
        @pl.loop(0, groups_of(lists_ref[j, 0] & 63))
        def _(g):
            action(
                pltpu.make_async_copy(
                    vals_ref.at[pl.ds(pl.multiple_of(j * SLOTS + g * GROUP, GROUP), GROUP)],
                    vals.at[pl.ds(pl.multiple_of(k * SLOTS + g * GROUP, GROUP), GROUP)],
                    sems.at[k * GROUPS + g],
                )
            )

    return each


def add_list(panel, piece, vals, lists_ref, j, k, wait=None):
    count = lists_ref[j, 0] & 63

    @pl.loop(0, groups_of(count))
    def _(g):
        if wait is not None:
            wait(g)
        products, rows = [], []
        for u in range(GROUP):
            q = g * GROUP + u
            entry = jnp.where(q < count, lists_ref[j, q] >> 6, PANEL_BLK * 4)
            rows.append(pl.ds(pl.multiple_of((entry >> 2) * BS, BS), BS))
            products.append(
                jnp.dot(
                    vals[k * SLOTS + q],
                    piece[pl.ds(pl.multiple_of((entry & 3) * BS, BS), BS), :],
                    preferred_element_type=jnp.float32,
                )
            )
        for row, product in zip(rows, products):
            panel[row, :] += product


def group_wait(vals_ref, vals, sems, j, k):
    def wait(g):
        pltpu.make_async_copy(
            vals_ref.at[pl.ds(pl.multiple_of(j * SLOTS + g * GROUP, GROUP), GROUP)],
            vals.at[pl.ds(pl.multiple_of(k * SLOTS + g * GROUP, GROUP), GROUP)],
            sems.at[k * GROUPS + g],
        ).wait()

    return wait


def piece_of(shift, flip):
    place = lax.axis_index("blk")
    x_hi = lax.rem(place, 2)
    return lax.rem(lax.div(place, 2) + shift, 4) * 2 + (1 - x_hi if flip else x_hi)


def hold(own_ref, out_ref):
    out_ref[...] = own_ref[...]


def first_products(which, ahead, lists_ref, own_ref, flipped_ref, vals_ref, panel, next_vals, *scratch):
    vals, sems, next_sems = scratch
    todo = [piece_of(*piece) for piece in which]
    for k, j in enumerate(todo):
        fetch(vals_ref, vals, sems, lists_ref, j, k)(lambda copy: copy.start())
    later = [
        fetch(vals_ref, next_vals, next_sems, lists_ref, piece_of(*piece), k) for k, piece in enumerate(ahead)
    ]
    for each in later:
        each(lambda copy: copy.start())

    @pl.loop(0, PANEL_BLK // 4)
    def _(k):
        panel[pl.ds(pl.multiple_of(k * 4 * BS, 4 * BS), 4 * BS), :] = jnp.zeros((4 * BS, F), jnp.float32)

    for k, (j, piece) in enumerate(zip(todo, (own_ref, flipped_ref))):
        add_list(panel, piece, vals, lists_ref, j, k, group_wait(vals_ref, vals, sems, j, k))
    for each in later:
        each(lambda copy: copy.wait())


def more_products(pieces, first, lists_ref, _, vals, *refs):
    *arrays, panel = refs
    for k, (piece, array) in enumerate(zip(pieces, arrays)):
        add_list(panel, array, vals, lists_ref, piece_of(*piece), first + k)


def quantize(block):
    peak = jnp.maximum(jnp.max(jnp.abs(block), axis=0, keepdims=True), 1e-32)
    exponent = jnp.ceil(jnp.log2(peak) + 0.001)
    scaled = block * (jnp.exp2(-exponent) * TOP)
    return jnp.round(scaled).astype(jnp.int32).astype(jnp.int16), exponent


def messages(count, part):
    return jax.ShapeDtypeStruct((count * part[1] * part[2] + 16, F), jnp.int16)


def write_messages(out_ref, part, values):
    _, rows, count = part
    row = lax.broadcasted_iota(jnp.int32, (16, F), 0)
    tail = jnp.zeros((16, F), jnp.float32)
    k = 0
    for value in values:
        for block in value():
            whole, exponent = quantize(block)
            out_ref[k * rows : (k + 1) * rows, :] = whole
            tail = jnp.where(row == k, exponent, tail)
            k += 1
    out_ref[k * rows : k * rows + 16, :] = tail.astype(jnp.int32).astype(jnp.int16)


def read_message(ref, index, part):
    _, rows, count = part
    last = ref.shape[0] - 16
    row = lax.broadcasted_iota(jnp.int32, (16, F), 0)
    tail = ref[last : last + 16, :].astype(jnp.int32).astype(jnp.float32)
    blocks = []
    for i in range(count):
        k = index * count + i
        if isinstance(k, int):
            exponent = tail[k : k + 1, :]
            whole = ref[k * rows : (k + 1) * rows, :]
        else:
            exponent = jnp.sum(jnp.where(row == k, tail, 0.0), axis=0, keepdims=True)
            whole = ref[pl.ds(pl.multiple_of(k * rows, 16), rows), :]
        blocks.append(whole.astype(jnp.int32).astype(jnp.float32) * (jnp.exp2(exponent) * (1.0 / TOP)))
    return blocks


def add(first, *others):
    for other in others:
        first = [a + b for a, b in zip(first, other)]
    return first


class Here:
    def __init__(self, panel=None):
        place = lax.axis_index("rep")
        self.core, self.x, self.z = lax.rem(place, 2), lax.div(place, 16), lax.rem(lax.div(place, 2), 8)
        self.panel = panel

    def z_of(self, shift):
        return lax.rem(self.z + shift + 8, 8)

    def partial(self, other_x, z, part, other_core=False):
        start, rows, count = part
        core = 1 - self.core if other_core else self.core
        owner = (1 - self.x if other_x else self.x) * 16 + z * 2 + core
        base = owner * PIECE_ROWS + start
        return [self.panel[pl.ds(pl.multiple_of(base + i * rows, 16), rows), :] for i in range(count)]


def core_messages(part, other_x, panel, out_ref):
    here = Here(panel)
    write_messages(
        out_ref, part,
        [
            functools.partial(here.partial, other, z, part, other_core=True)
            for other in other_x for z in range(8)
        ],
    )


def last_products(pieces, first, *refs):
    more_products(pieces, first, *refs[:-1])
    core_messages(FIRST, (True,), *refs[-2:])


def rest_to_core(panel, out_ref):
    core_messages(SECOND, (False, True), panel, core_part(out_ref, SECOND))
    core_messages(FIRST, (False,), panel, core_part(out_ref, FIRST))


def core_part(ref, part):
    second_rows, first_rows = messages(16, SECOND).shape[0], messages(8, FIRST).shape[0]
    return ref.at[pl.ds(0, second_rows)] if part == SECOND else ref.at[pl.ds(second_rows, first_rows)]


def x_messages(panel, rc_ref, out_ref):
    here = Here(panel)
    write_messages(
        out_ref, FIRST,
        [lambda z=z: add(here.partial(True, z, FIRST), read_message(rc_ref, z, FIRST)) for z in range(8)],
    )


def base_value(part, here, rc_ref, rx_ref, other, z):
    value = add(here.partial(other, z, part), read_message(core_part(rc_ref, part), other * 8 + z, part))
    return value if rx_ref is None else add(value, read_message(rx_ref, z, part))


def sides(part):
    return (0,) if part == FIRST else (0, 1)


def z_start(part, panel, rc_ref, rx_ref, down_ref, up_ref, two_ref):
    here = Here(panel)
    for out_ref, shifts in ((down_ref, (-4, -1)), (up_ref, (2,)), (two_ref, (-2,))):
        write_messages(
            out_ref, part,
            [
                functools.partial(base_value, part, here, rc_ref, rx_ref, other, here.z_of(shift))
                for other in sides(part) for shift in shifts
            ],
        )


def z_middle(part, panel, rc_ref, rx_ref, down_ref, up_ref, three_ref, one_ref, far_ref):
    here = Here(panel)

    def through(come_ref, stride, shift):
        return [
            lambda other=other: add(
                base_value(part, here, rc_ref, rx_ref, other, here.z_of(shift)),
                read_message(come_ref, stride * other, part),
            )
            for other in sides(part)
        ]

    write_messages(three_ref, part, through(down_ref, 2, -3))
    write_messages(one_ref, part, through(up_ref, 1, 1))
    write_messages(
        far_ref, part,
        [functools.partial(base_value, part, here, rc_ref, rx_ref, other, here.z_of(3)) for other in sides(part)],
    )


def arrivals(part, other, down_ref, *refs):
    return [read_message(down_ref, 2 * other + 1, part)] + [read_message(ref, other, part) for ref in refs]


def z_end(panel, rc_ref, *refs):
    here = Here(panel)
    *arrived, out_ref, sum_ref = refs
    value = base_value(SECOND, here, rc_ref, None, 1, here.z)
    write_messages(out_ref, SECOND, [lambda: add(value, *arrivals(SECOND, 1, *arrived))])
    mine = base_value(SECOND, here, rc_ref, None, 0, here.z)
    sum_ref[...] = add(mine, *arrivals(SECOND, 0, *arrived))[0]


def layer(panel, rc_ref, rx_ref, sum_ref, rx2_ref, *refs):
    here = Here(panel)
    *arrived, weight_ref, out_ref = refs
    first = add(base_value(FIRST, here, rc_ref, rx_ref, 0, here.z), *arrivals(FIRST, 0, *arrived))
    second = add([sum_ref[...]], read_message(rx2_ref, 0, SECOND))
    weight = weight_ref[...]
    row = 0
    for block in first + second:
        high = block.astype(jnp.bfloat16)
        rest = block - high.astype(jnp.float32)
        middle = rest.astype(jnp.bfloat16)
        low = (rest - middle.astype(jnp.float32)).astype(jnp.bfloat16)
        result = jnp.dot(low, weight, preferred_element_type=jnp.float32)
        result += jnp.dot(middle, weight, preferred_element_type=jnp.float32)
        result += jnp.dot(high, weight, preferred_element_type=jnp.float32)
        out_ref[row : row + block.shape[0], :] = jnp.maximum(result, 0.0).astype(jnp.bfloat16)
        row += block.shape[0]


def send_blk(array, dy, flip=0):
    pairs = [(y * 2 + h, ((y + dy) % 4) * 2 + (h ^ flip)) for y in range(4) for h in range(2)]
    return lax.ppermute(array, "blk", pairs)


def send_rep(array, dx, dz, dc):
    pairs = [
        (x * 16 + z * 2 + c, (x ^ dx) * 16 + ((z + dz) % 8) * 2 + (c ^ dc))
        for x in range(2) for z in range(8) for c in range(2)
    ]
    return lax.ppermute(array, "rep", pairs)


def sum_along_z(part, name, panel, rc, rx):
    count = len(sides(part))
    have = (rc,) if rx is None else (rc, rx)

    def fill(kernel):
        if rx is not None:
            return functools.partial(kernel, part)
        return lambda panel_ref, rc_ref, *refs: kernel(part, panel_ref, rc_ref, None, *refs)

    down, up, two = call(
        fill(z_start), name + "_start", (messages(2 * count, part),) + (messages(count, part),) * 2,
        [VMEM] * (1 + len(have)), (VMEM,) * 3, (panel, *have), 0.6,
    )
    down, up = send_rep(down, 0, -1, 0), send_rep(up, 0, 1, 0)
    two = send_rep(two, 0, -2, 0)
    three, one, far = call(
        fill(z_middle), name + "_middle", (messages(count, part),) * 3,
        [VMEM] * (3 + len(have)), (VMEM,) * 3, (panel, *have, down, up), 0.6,
    )
    return down, two, send_rep(far, 0, 3, 0), send_rep(three, 0, -3, 0), send_rep(one, 0, 1, 0)


def local(node_feats, block_vals, block_rows, block_cols, block_count, weight):
    vals = block_vals.reshape(LISTS * SLOTS, BS, BS)
    panel_type = jax.ShapeDtypeStruct(((PANEL_BLK + 1) * BS, F), jnp.float32)
    here, near, far = ((0, False), (0, True)), ((3, False), (1, False), (3, True), (1, True), (2, False)), ((2, True),)
    own = node_feats
    flipped, below, above = send_blk(own, 0, 1), send_blk(own, 1), send_blk(own, -1)
    own = call(hold, "own_piece", jax.ShapeDtypeStruct((PIECE_ROWS, F), jnp.bfloat16), [VMEM], VMEM, (own,), 1)
    slots = block_rows.reshape(LISTS, SLOTS) * 4 + block_cols.reshape(LISTS, SLOTS)
    lists = slots * 64 + block_count.reshape(LISTS, 1)
    flipped, own, lists = lax.optimization_barrier((flipped, own, lists))
    below_flipped, above_flipped, far_own = send_blk(flipped, 1), send_blk(flipped, -1), send_blk(below, 1)
    later = len(near) + len(far)
    panel, next_vals = call(
        functools.partial(first_products, here, near + far), "products_here",
        (panel_type, jax.ShapeDtypeStruct((later * SLOTS, BS, BS), jnp.bfloat16)),
        [SMEM, VMEM, VMEM, ANY], (VMEM,) * 2, (lists, own, flipped, vals), 4, 40,
        scratch_shapes=[
            pltpu.VMEM((2 * SLOTS, BS, BS), jnp.bfloat16),
            pltpu.SemaphoreType.DMA((2 * GROUPS,)),
            pltpu.SemaphoreType.DMA((later * GROUPS,)),
        ],
    )
    panel, above, below_flipped, above_flipped, far_own = lax.optimization_barrier(
        (panel, above, below_flipped, above_flipped, far_own)
    )
    far_flipped = send_blk(above_flipped, -1)
    panel = call(
        functools.partial(more_products, near, 0), "products_near", panel_type,
        [SMEM] + [VMEM] * 7, VMEM,
        (lists, panel, next_vals, below, above, below_flipped, above_flipped, far_own), 3, 24,
        input_output_aliases={1: 0},
    )
    panel, to_core = call(
        functools.partial(last_products, far, len(near)), "products_far", (panel_type, messages(8, FIRST)),
        [SMEM] + [VMEM] * 3, (VMEM,) * 2, (lists, panel, next_vals, far_flipped), 3, 24,
        input_output_aliases={1: 0},
    )

    rc_cross = send_rep(to_core, 0, 0, 1)
    second_rows, first_rows = messages(16, SECOND).shape[0], messages(8, FIRST).shape[0]
    to_core = call(
        rest_to_core, "core_rest", jax.ShapeDtypeStruct((second_rows + first_rows, F), jnp.int16),
        [VMEM], VMEM, (panel,), 0.3,
    )
    rc = send_rep(to_core, 0, 0, 1)
    to_x = call(x_messages, "x_first", messages(8, FIRST), [VMEM, VMEM], VMEM, (panel, rc_cross), 0.6)
    rx_first = send_rep(to_x, 1, 0, 0)
    second = sum_along_z(SECOND, "second", panel, rc, None)
    to_x, own_sum = call(
        z_end, "x_second", (messages(1, SECOND), jax.ShapeDtypeStruct((SECOND[1], F), jnp.float32)),
        [VMEM] * 7, (VMEM,) * 2, (panel, rc, *second), 0.6,
    )
    panel, to_x = lax.optimization_barrier((panel, to_x))
    rx_second = send_rep(to_x, 1, 0, 0)
    first = sum_along_z(FIRST, "first", panel, rc, rx_first)
    return call(
        layer, "layer", jax.ShapeDtypeStruct((PIECE_ROWS, H), jnp.bfloat16), [VMEM] * 11, VMEM,
        (panel, rc, rx_first, own_sum, rx_second, *first, weight), 1.5,
    )


def solution(mesh):
    return jax.shard_map(
        local,
        mesh=mesh,
        in_specs=(
            P(("blk", "rep"), None),
            P("blk", "rep", None, None, None, None),
            P("blk", "rep", None, None),
            P("blk", "rep", None, None),
            P("blk", "rep", None),
            P(),
        ),
        out_specs=P(("blk", "rep"), None),
        check_vma=False,
    )
```

```python
import functools

import jax
import jax.numpy as jnp
from jax import lax
from jax.experimental import pallas as pl
from jax.experimental.pallas import tpu as pltpu
from jax.sharding import PartitionSpec as P

BS = 128
F = 128
H = 256
SLOTS = 40
LISTS = 8
PIECE_BLK = 3
PIECE_ROWS = PIECE_BLK * BS
HALF = PIECE_ROWS // 2
PANEL_BLK = 96
GROUP = 8
GROUPS = SLOTS // GROUP
TOP = 32766.0
MIB = 1 << 20

FIRST, SECOND = (0, 144, 2), (288, 96, 1)


SMEM = pl.BlockSpec(memory_space=pltpu.SMEM)
VMEM = pl.BlockSpec(memory_space=pltpu.VMEM)
ANY = pl.BlockSpec(memory_space=pl.ANY)


def call(kernel, name, out_shape, in_specs, out_specs, args, us, mib=24, **more):
    return pl.pallas_call(
        kernel,
        out_shape=out_shape,
        in_specs=in_specs,
        out_specs=out_specs,
        compiler_params=pltpu.CompilerParams(vmem_limit_bytes=mib * MIB),
        cost_estimate=pl.CostEstimate(flops=0, bytes_accessed=int(us * 3.0e6), transcendentals=0),
        name=name,
        **more,
    )(*args)


def groups_of(count):
    return lax.div(jnp.clip(count, 0, SLOTS) + (GROUP - 1), GROUP)


def fetch(vals_ref, vals, sems, lists_ref, j, k):
    def each(action):
        @pl.loop(0, groups_of(lists_ref[j, 0] & 63))
        def _(g):
            action(
                pltpu.make_async_copy(
                    vals_ref.at[pl.ds(pl.multiple_of(j * SLOTS + g * GROUP, GROUP), GROUP)],
                    vals.at[pl.ds(pl.multiple_of(k * SLOTS + g * GROUP, GROUP), GROUP)],
                    sems.at[k * GROUPS + g],
                )
            )

    return each


def add_list(panel, piece, vals, lists_ref, j, k, wait=None):
    count = lists_ref[j, 0] & 63
    groups = groups_of(count)

    def add_groups(g, many):
        if wait is not None:
            for i in range(many):
                wait(g + i)
        products, rows = [], []
        for u in range(many * GROUP):
            q = g * GROUP + u
            entry = jnp.where(q < count, lists_ref[j, q] >> 6, PANEL_BLK * 4)
            rows.append(pl.ds(pl.multiple_of((entry >> 2) * BS, BS), BS))
            products.append(
                jnp.dot(
                    vals[k * SLOTS + q],
                    piece[pl.ds(pl.multiple_of((entry & 3) * BS, BS), BS), :],
                    preferred_element_type=jnp.float32,
                )
            )
        for row, product in zip(rows, products):
            panel[row, :] += product

    @pl.loop(0, lax.div(groups, 2))
    def _(pair):
        add_groups(2 * pair, 2)

    @pl.when(lax.rem(groups, 2) == 1)
    def _():
        add_groups(groups - 1, 1)


def add_lists(panel, arrays, pieces, vals, lists_ref, which, wait=None):
    for k, array in enumerate(arrays):
        pieces[k] = array[...]

    @pl.loop(0, len(which))
    def _(k):
        j = piece_of(*which[0])
        for i, piece in enumerate(which[1:], 1):
            j = jnp.where(k == i, piece_of(*piece), j)
        add_list(panel, pieces.at[k], vals, lists_ref, j, k, wait and wait(j, k))


def group_wait(vals_ref, vals, sems, j, k):
    def wait(g):
        pltpu.make_async_copy(
            vals_ref.at[pl.ds(pl.multiple_of(j * SLOTS + g * GROUP, GROUP), GROUP)],
            vals.at[pl.ds(pl.multiple_of(k * SLOTS + g * GROUP, GROUP), GROUP)],
            sems.at[k * GROUPS + g],
        ).wait()

    return wait


def piece_of(shift, flip):
    place = lax.axis_index("blk")
    x_hi = lax.rem(place, 2)
    return lax.rem(lax.div(place, 2) + shift, 4) * 2 + (1 - x_hi if flip else x_hi)


def hold(own_ref, out_ref):
    out_ref[...] = own_ref[...]


def first_products(which, ahead, lists_ref, own_ref, flipped_ref, vals_ref, panel, next_vals, *scratch):
    pieces, vals, sems, next_sems = scratch
    todo = [piece_of(*piece) for piece in which]
    for k, j in enumerate(todo):
        fetch(vals_ref, vals, sems, lists_ref, j, k)(lambda copy: copy.start())
    later = [
        fetch(vals_ref, next_vals, next_sems, lists_ref, piece_of(*piece), k) for k, piece in enumerate(ahead)
    ]
    for each in later:
        each(lambda copy: copy.start())

    @pl.loop(0, PANEL_BLK // 4)
    def _(k):
        panel[pl.ds(pl.multiple_of(k * 4 * BS, 4 * BS), 4 * BS), :] = jnp.zeros((4 * BS, F), jnp.float32)

    add_lists(
        panel, (own_ref, flipped_ref), pieces, vals, lists_ref, which,
        functools.partial(group_wait, vals_ref, vals, sems),
    )
    for each in later:
        each(lambda copy: copy.wait())


def more_products(which, lists_ref, _, vals, *refs):
    *arrays, panel, pieces = refs
    add_lists(panel, arrays, pieces, vals, lists_ref, which)


def quantize(block):
    peak = jnp.maximum(jnp.max(jnp.abs(block), axis=0, keepdims=True), 1e-32)
    exponent = jnp.ceil(jnp.log2(peak) + 0.001)
    scaled = block * (jnp.exp2(-exponent) * TOP)
    return jnp.round(scaled).astype(jnp.int32).astype(jnp.int16), exponent


def messages(count, part):
    return jax.ShapeDtypeStruct((count * part[1] * part[2] + 16, F), jnp.int16)


def write_messages(out_ref, part, values):
    _, rows, count = part
    row = lax.broadcasted_iota(jnp.int32, (16, F), 0)
    tail = jnp.zeros((16, F), jnp.float32)
    k = 0
    for value in values:
        for block in value():
            whole, exponent = quantize(block)
            out_ref[k * rows : (k + 1) * rows, :] = whole
            tail = jnp.where(row == k, exponent, tail)
            k += 1
    out_ref[k * rows : k * rows + 16, :] = tail.astype(jnp.int32).astype(jnp.int16)


def read_message(ref, index, part):
    _, rows, count = part
    last = ref.shape[0] - 16
    row = lax.broadcasted_iota(jnp.int32, (16, F), 0)
    tail = ref[last : last + 16, :].astype(jnp.int32).astype(jnp.float32)
    blocks = []
    for i in range(count):
        k = index * count + i
        if isinstance(k, int):
            exponent = tail[k : k + 1, :]
            whole = ref[k * rows : (k + 1) * rows, :]
        else:
            exponent = jnp.sum(jnp.where(row == k, tail, 0.0), axis=0, keepdims=True)
            whole = ref[pl.ds(pl.multiple_of(k * rows, 16), rows), :]
        blocks.append(whole.astype(jnp.int32).astype(jnp.float32) * (jnp.exp2(exponent) * (1.0 / TOP)))
    return blocks


def add(first, *others):
    for other in others:
        first = [a + b for a, b in zip(first, other)]
    return first


class Here:
    def __init__(self, panel=None):
        place = lax.axis_index("rep")
        self.core, self.x, self.z = lax.rem(place, 2), lax.div(place, 16), lax.rem(lax.div(place, 2), 8)
        self.panel = panel

    def z_of(self, shift):
        return lax.rem(self.z + shift + 8, 8)

    def partial(self, other_x, z, part, other_core=False):
        start, rows, count = part
        core = 1 - self.core if other_core else self.core
        owner = (1 - self.x if other_x else self.x) * 16 + z * 2 + core
        base = owner * PIECE_ROWS + start
        return [self.panel[pl.ds(pl.multiple_of(base + i * rows, 16), rows), :] for i in range(count)]


def core_messages(part, other_x, panel, out_ref):
    here = Here(panel)
    write_messages(
        out_ref, part,
        [
            functools.partial(here.partial, other, z, part, other_core=True)
            for other in other_x for z in range(8)
        ],
    )


def last_products(which, place, lists_ref, _, vals, piece, panel, out_ref):
    add_list(panel, piece, vals, lists_ref, piece_of(*which), place)
    core_messages(FIRST, (True,), panel, out_ref)


def rest_to_core(panel, out_ref):
    core_messages(SECOND, (False, True), panel, core_part(out_ref, SECOND))
    core_messages(FIRST, (False,), panel, core_part(out_ref, FIRST))


def core_part(ref, part):
    second_rows, first_rows = messages(16, SECOND).shape[0], messages(8, FIRST).shape[0]
    return ref.at[pl.ds(0, second_rows)] if part == SECOND else ref.at[pl.ds(second_rows, first_rows)]


def x_messages(panel, rc_ref, out_ref):
    here = Here(panel)
    write_messages(
        out_ref, FIRST,
        [lambda z=z: add(here.partial(True, z, FIRST), read_message(rc_ref, z, FIRST)) for z in range(8)],
    )


def base_value(part, here, rc_ref, rx_ref, other, z):
    value = add(here.partial(other, z, part), read_message(core_part(rc_ref, part), other * 8 + z, part))
    return value if rx_ref is None else add(value, read_message(rx_ref, z, part))


def sides(part):
    return (0,) if part == FIRST else (0, 1)


def z_start(part, panel, rc_ref, rx_ref, down_ref, up_ref, two_ref, far_ref):
    here = Here(panel)
    for out_ref, shifts in ((down_ref, (-4, -1)), (up_ref, (2,)), (two_ref, (-2,)), (far_ref, (3,))):
        write_messages(
            out_ref, part,
            [
                functools.partial(base_value, part, here, rc_ref, rx_ref, other, here.z_of(shift))
                for other in sides(part) for shift in shifts
            ],
        )


def z_middle(part, panel, rc_ref, rx_ref, down_ref, up_ref, three_ref, one_ref):
    here = Here(panel)

    def through(come_ref, stride, shift):
        return [
            lambda other=other: add(
                base_value(part, here, rc_ref, rx_ref, other, here.z_of(shift)),
                read_message(come_ref, stride * other, part),
            )
            for other in sides(part)
        ]

    write_messages(three_ref, part, through(down_ref, 2, -3))
    write_messages(one_ref, part, through(up_ref, 1, 1))


def arrivals(part, other, down_ref, *refs):
    return [read_message(down_ref, 2 * other + 1, part)] + [read_message(ref, other, part) for ref in refs]


def z_end(panel, rc_ref, *refs):
    here = Here(panel)
    *arrived, out_ref, sum_ref = refs
    value = base_value(SECOND, here, rc_ref, None, 1, here.z)
    write_messages(out_ref, SECOND, [lambda: add(value, *arrivals(SECOND, 1, *arrived))])
    mine = base_value(SECOND, here, rc_ref, None, 0, here.z)
    sum_ref[...] = add(mine, *arrivals(SECOND, 0, *arrived))[0]


def layer(panel, rc_ref, rx_ref, sum_ref, rx2_ref, *refs):
    here = Here(panel)
    *arrived, weight_ref, out_ref = refs
    first = add(base_value(FIRST, here, rc_ref, rx_ref, 0, here.z), *arrivals(FIRST, 0, *arrived))
    second = add([sum_ref[...]], read_message(rx2_ref, 0, SECOND))
    weight = weight_ref[...]
    row = 0
    for block in first + second:
        high = block.astype(jnp.bfloat16)
        rest = block - high.astype(jnp.float32)
        middle = rest.astype(jnp.bfloat16)
        low = (rest - middle.astype(jnp.float32)).astype(jnp.bfloat16)
        result = jnp.dot(low, weight, preferred_element_type=jnp.float32)
        result += jnp.dot(middle, weight, preferred_element_type=jnp.float32)
        result += jnp.dot(high, weight, preferred_element_type=jnp.float32)
        out_ref[row : row + block.shape[0], :] = jnp.maximum(result, 0.0).astype(jnp.bfloat16)
        row += block.shape[0]


def send_blk(array, dy, flip=0):
    pairs = [(y * 2 + h, ((y + dy) % 4) * 2 + (h ^ flip)) for y in range(4) for h in range(2)]
    return lax.ppermute(array, "blk", pairs)


def send_rep(array, dx, dz, dc):
    pairs = [
        (x * 16 + z * 2 + c, (x ^ dx) * 16 + ((z + dz) % 8) * 2 + (c ^ dc))
        for x in range(2) for z in range(8) for c in range(2)
    ]
    return lax.ppermute(array, "rep", pairs)


def sum_along_z(part, name, panel, rc, rx):
    count = len(sides(part))
    have = (rc,) if rx is None else (rc, rx)

    def fill(kernel):
        if rx is not None:
            return functools.partial(kernel, part)
        return lambda panel_ref, rc_ref, *refs: kernel(part, panel_ref, rc_ref, None, *refs)

    down, up, two, far = call(
        fill(z_start), name + "_start", (messages(2 * count, part),) + (messages(count, part),) * 3,
        [VMEM] * (1 + len(have)), (VMEM,) * 4, (panel, *have), 0.6,
    )
    down, up = send_rep(down, 0, -1, 0), send_rep(up, 0, 1, 0)
    two, far = send_rep(two, 0, -2, 0), send_rep(far, 0, 3, 0)
    three, one = call(
        fill(z_middle), name + "_middle", (messages(count, part),) * 2,
        [VMEM] * (3 + len(have)), (VMEM,) * 2, (panel, *have, down, up), 0.6,
    )
    return down, two, far, send_rep(three, 0, -3, 0), send_rep(one, 0, 1, 0)


def local(node_feats, block_vals, block_rows, block_cols, block_count, weight):
    vals = block_vals.reshape(LISTS * SLOTS, BS, BS)
    panel_type = jax.ShapeDtypeStruct(((PANEL_BLK + 1) * BS, F), jnp.float32)
    here, near, far = ((0, False), (0, True)), ((3, False), (1, False), (3, True), (1, True), (2, False)), ((2, True),)
    own = node_feats
    flipped, below, above = send_blk(own, 0, 1), send_blk(own, 1), send_blk(own, -1)
    own = call(hold, "own_piece", jax.ShapeDtypeStruct((PIECE_ROWS, F), jnp.bfloat16), [VMEM], VMEM, (own,), 1)
    slots = block_rows.reshape(LISTS, SLOTS) * 4 + block_cols.reshape(LISTS, SLOTS)
    lists = slots * 64 + block_count.reshape(LISTS, 1)
    flipped, own, lists = lax.optimization_barrier((flipped, own, lists))
    below_flipped, above_flipped, far_own = send_blk(flipped, 1), send_blk(flipped, -1), send_blk(below, 1)
    later = len(near) + len(far)
    panel, next_vals = call(
        functools.partial(first_products, here, near + far), "products_here",
        (panel_type, jax.ShapeDtypeStruct((later * SLOTS, BS, BS), jnp.bfloat16)),
        [SMEM, VMEM, VMEM, ANY], (VMEM,) * 2, (lists, own, flipped, vals), 4, 40,
        scratch_shapes=[
            pltpu.VMEM((len(here), PIECE_ROWS, F), jnp.bfloat16),
            pltpu.VMEM((2 * SLOTS, BS, BS), jnp.bfloat16),
            pltpu.SemaphoreType.DMA((2 * GROUPS,)),
            pltpu.SemaphoreType.DMA((later * GROUPS,)),
        ],
    )
    panel, above, below_flipped, above_flipped, far_own = lax.optimization_barrier(
        (panel, above, below_flipped, above_flipped, far_own)
    )
    far_flipped = send_blk(above_flipped, -1)
    panel = call(
        functools.partial(more_products, near), "products_near", panel_type,
        [SMEM] + [VMEM] * 7, VMEM,
        (lists, panel, next_vals, below, above, below_flipped, above_flipped, far_own), 3, 24,
        input_output_aliases={1: 0},
        scratch_shapes=[pltpu.VMEM((len(near), PIECE_ROWS, F), jnp.bfloat16)],
    )
    panel, to_core = call(
        functools.partial(last_products, far[0], len(near)), "products_far", (panel_type, messages(8, FIRST)),
        [SMEM] + [VMEM] * 3, (VMEM,) * 2, (lists, panel, next_vals, far_flipped), 3, 24,
        input_output_aliases={1: 0},
    )

    rc_cross = send_rep(to_core, 0, 0, 1)
    second_rows, first_rows = messages(16, SECOND).shape[0], messages(8, FIRST).shape[0]
    to_core = call(
        rest_to_core, "core_rest", jax.ShapeDtypeStruct((second_rows + first_rows, F), jnp.int16),
        [VMEM], VMEM, (panel,), 0.3,
    )
    rc = send_rep(to_core, 0, 0, 1)
    to_x = call(x_messages, "x_first", messages(8, FIRST), [VMEM, VMEM], VMEM, (panel, rc_cross), 0.6)
    rx_first = send_rep(to_x, 1, 0, 0)
    second = sum_along_z(SECOND, "second", panel, rc, None)
    to_x, own_sum = call(
        z_end, "x_second", (messages(1, SECOND), jax.ShapeDtypeStruct((SECOND[1], F), jnp.float32)),
        [VMEM] * 7, (VMEM,) * 2, (panel, rc, *second), 0.6,
    )
    panel, to_x = lax.optimization_barrier((panel, to_x))
    rx_second = send_rep(to_x, 1, 0, 0)
    first = sum_along_z(FIRST, "first", panel, rc, rx_first)
    return call(
        layer, "layer", jax.ShapeDtypeStruct((PIECE_ROWS, H), jnp.bfloat16), [VMEM] * 11, VMEM,
        (panel, rc, rx_first, own_sum, rx_second, *first, weight), 1.5,
    )


def solution(mesh):
    return jax.shard_map(
        local,
        mesh=mesh,
        in_specs=(
            P(("blk", "rep"), None),
            P("blk", "rep", None, None, None, None),
            P("blk", "rep", None, None),
            P("blk", "rep", None, None),
            P("blk", "rep", None),
            P(),
        ),
        out_specs=P(("blk", "rep"), None),
        check_vma=False,
    )
```

```python
import functools

import jax
import jax.numpy as jnp
from jax import lax
from jax.experimental import pallas as pl
from jax.experimental.pallas import tpu as pltpu
from jax.sharding import PartitionSpec as P

BS = 128
F = 128
H = 256
SLOTS = 40
LISTS = 8
PIECE_BLK = 3
PIECE_ROWS = PIECE_BLK * BS
HALF = PIECE_ROWS // 2
PANEL_BLK = 96
GROUP = 8
GROUPS = SLOTS // GROUP
TOP = 32766.0
MIB = 1 << 20

FIRST, SECOND = (0, 144, 2), (288, 96, 1)


SMEM = pl.BlockSpec(memory_space=pltpu.SMEM)
VMEM = pl.BlockSpec(memory_space=pltpu.VMEM)
ANY = pl.BlockSpec(memory_space=pl.ANY)


def call(kernel, name, out_shape, in_specs, out_specs, args, us, mib=24, **more):
    return pl.pallas_call(
        kernel,
        out_shape=out_shape,
        in_specs=in_specs,
        out_specs=out_specs,
        compiler_params=pltpu.CompilerParams(vmem_limit_bytes=mib * MIB),
        cost_estimate=pl.CostEstimate(flops=0, bytes_accessed=int(us * 3.0e6), transcendentals=0),
        name=name,
        **more,
    )(*args)


def groups_of(count):
    return lax.div(jnp.clip(count, 0, SLOTS) + (GROUP - 1), GROUP)


def fetch(vals_ref, vals, sems, lists_ref, j, k):
    def each(action):
        @pl.loop(0, groups_of(lists_ref[j, 0] & 63))
        def _(g):
            action(
                pltpu.make_async_copy(
                    vals_ref.at[pl.ds(pl.multiple_of(j * SLOTS + g * GROUP, GROUP), GROUP)],
                    vals.at[pl.ds(pl.multiple_of(k * SLOTS + g * GROUP, GROUP), GROUP)],
                    sems.at[k * GROUPS + g],
                )
            )

    return each


def add_list(panel, piece, vals, lists_ref, j, k, wait=None):
    count = lists_ref[j, 0] & 63
    groups = groups_of(count)

    def add_groups(g, many):
        if wait is not None:
            for i in range(many):
                wait(g + i)
        products, rows = [], []
        for u in range(many * GROUP):
            q = g * GROUP + u
            entry = jnp.where(q < count, lists_ref[j, q] >> 6, PANEL_BLK * 4)
            rows.append(pl.ds(pl.multiple_of((entry >> 2) * BS, BS), BS))
            products.append(
                jnp.dot(
                    vals[k * SLOTS + q],
                    piece[pl.ds(pl.multiple_of((entry & 3) * BS, BS), BS), :],
                    preferred_element_type=jnp.float32,
                )
            )
        for row, product in zip(rows, products):
            panel[row, :] += product

    @pl.loop(0, lax.div(groups, 2))
    def _(pair):
        add_groups(2 * pair, 2)

    @pl.when(lax.rem(groups, 2) == 1)
    def _():
        add_groups(groups - 1, 1)


def add_lists(panel, arrays, pieces, vals, lists_ref, which, wait=None):
    for k, array in enumerate(arrays):
        pieces[k] = array[...]

    @pl.loop(0, len(which))
    def _(k):
        j = piece_of(*which[0])
        for i, piece in enumerate(which[1:], 1):
            j = jnp.where(k == i, piece_of(*piece), j)
        add_list(panel, pieces.at[k], vals, lists_ref, j, k, wait and wait(j, k))


def group_wait(vals_ref, vals, sems, j, k):
    def wait(g):
        pltpu.make_async_copy(
            vals_ref.at[pl.ds(pl.multiple_of(j * SLOTS + g * GROUP, GROUP), GROUP)],
            vals.at[pl.ds(pl.multiple_of(k * SLOTS + g * GROUP, GROUP), GROUP)],
            sems.at[k * GROUPS + g],
        ).wait()

    return wait


def piece_of(shift, flip):
    place = lax.axis_index("blk")
    x_hi = lax.rem(place, 2)
    return lax.rem(lax.div(place, 2) + shift, 4) * 2 + (1 - x_hi if flip else x_hi)


def hold(own_ref, out_ref):
    out_ref[...] = own_ref[...]


def first_products(which, ahead, lists_ref, own_ref, flipped_ref, vals_ref, panel, next_vals, *scratch):
    pieces, vals, sems, next_sems = scratch
    todo = [piece_of(*piece) for piece in which]
    for k, j in enumerate(todo):
        fetch(vals_ref, vals, sems, lists_ref, j, k)(lambda copy: copy.start())
    later = [
        fetch(vals_ref, next_vals, next_sems, lists_ref, piece_of(*piece), k) for k, piece in enumerate(ahead)
    ]
    for each in later:
        each(lambda copy: copy.start())

    @pl.loop(0, PANEL_BLK // 4)
    def _(k):
        panel[pl.ds(pl.multiple_of(k * 4 * BS, 4 * BS), 4 * BS), :] = jnp.zeros((4 * BS, F), jnp.float32)

    add_lists(
        panel, (own_ref, flipped_ref), pieces, vals, lists_ref, which,
        functools.partial(group_wait, vals_ref, vals, sems),
    )
    for each in later:
        each(lambda copy: copy.wait())


def more_products(which, lists_ref, _, vals, *refs):
    *arrays, panel, pieces = refs
    add_lists(panel, arrays, pieces, vals, lists_ref, which)


def quantize(block):
    peak = jnp.maximum(jnp.max(jnp.abs(block), axis=0, keepdims=True), 1e-32)
    exponent = jnp.ceil(jnp.log2(peak) + 0.001)
    scaled = block * (jnp.exp2(-exponent) * TOP)
    return jnp.round(scaled).astype(jnp.int32).astype(jnp.int16), exponent


def messages(count, part):
    return jax.ShapeDtypeStruct((count * part[1] * part[2] + 16, F), jnp.int16)


def write_messages(out_ref, part, values):
    _, rows, count = part
    row = lax.broadcasted_iota(jnp.int32, (16, F), 0)
    tail = jnp.zeros((16, F), jnp.float32)
    k = 0
    for value in values:
        for block in value():
            whole, exponent = quantize(block)
            out_ref[k * rows : (k + 1) * rows, :] = whole
            tail = jnp.where(row == k, exponent, tail)
            k += 1
    out_ref[k * rows : k * rows + 16, :] = tail.astype(jnp.int32).astype(jnp.int16)


def read_message(ref, index, part):
    _, rows, count = part
    last = ref.shape[0] - 16
    row = lax.broadcasted_iota(jnp.int32, (16, F), 0)
    tail = ref[last : last + 16, :].astype(jnp.int32).astype(jnp.float32)
    blocks = []
    for i in range(count):
        k = index * count + i
        if isinstance(k, int):
            exponent = tail[k : k + 1, :]
            whole = ref[k * rows : (k + 1) * rows, :]
        else:
            exponent = jnp.sum(jnp.where(row == k, tail, 0.0), axis=0, keepdims=True)
            whole = ref[pl.ds(pl.multiple_of(k * rows, 16), rows), :]
        blocks.append(whole.astype(jnp.int32).astype(jnp.float32) * (jnp.exp2(exponent) * (1.0 / TOP)))
    return blocks


def add(first, *others):
    for other in others:
        first = [a + b for a, b in zip(first, other)]
    return first


class Here:
    def __init__(self, panel=None):
        place = lax.axis_index("rep")
        self.core, self.x, self.z = lax.rem(place, 2), lax.div(place, 16), lax.rem(lax.div(place, 2), 8)
        self.panel = panel

    def z_of(self, shift):
        return lax.rem(self.z + shift + 8, 8)

    def partial(self, other_x, z, part, other_core=False):
        start, rows, count = part
        core = 1 - self.core if other_core else self.core
        owner = (1 - self.x if other_x else self.x) * 16 + z * 2 + core
        base = owner * PIECE_ROWS + start
        return [self.panel[pl.ds(pl.multiple_of(base + i * rows, 16), rows), :] for i in range(count)]


def core_messages(part, other_x, panel, out_ref):
    here = Here(panel)
    write_messages(
        out_ref, part,
        [
            functools.partial(here.partial, other, z, part, other_core=True)
            for other in other_x for z in range(8)
        ],
    )


def last_products(which, place, lists_ref, _, vals, piece, panel, out_ref):
    add_list(panel, piece, vals, lists_ref, piece_of(*which), place)
    core_messages(FIRST, (True,), panel, out_ref)


def rest_to_core(panel, out_ref):
    core_messages(SECOND, (False, True), panel, core_part(out_ref, SECOND))
    core_messages(FIRST, (False,), panel, core_part(out_ref, FIRST))


def core_part(ref, part):
    second_rows, first_rows = messages(16, SECOND).shape[0], messages(8, FIRST).shape[0]
    return ref.at[pl.ds(0, second_rows)] if part == SECOND else ref.at[pl.ds(second_rows, first_rows)]


def x_messages(panel, rc_ref, out_ref):
    here = Here(panel)
    write_messages(
        out_ref, FIRST,
        [lambda z=z: add(here.partial(True, z, FIRST), read_message(rc_ref, z, FIRST)) for z in range(8)],
    )


def base_value(part, here, rc_ref, rx_ref, other, z):
    value = add(here.partial(other, z, part), read_message(core_part(rc_ref, part), other * 8 + z, part))
    return value if rx_ref is None else add(value, read_message(rx_ref, z, part))


def sides(part):
    return (0,) if part == FIRST else (0, 1)


def z_start(part, panel, rc_ref, rx_ref, down_ref, up_ref, two_ref, far_ref):
    here = Here(panel)
    for out_ref, shifts in ((down_ref, (-4, -1)), (up_ref, (2,)), (two_ref, (-2,)), (far_ref, (3,))):
        write_messages(
            out_ref, part,
            [
                functools.partial(base_value, part, here, rc_ref, rx_ref, other, here.z_of(shift))
                for other in sides(part) for shift in shifts
            ],
        )


def z_middle(part, panel, rc_ref, rx_ref, down_ref, up_ref, three_ref, one_ref):
    here = Here(panel)

    def through(come_ref, stride, shift):
        return [
            lambda other=other: add(
                base_value(part, here, rc_ref, rx_ref, other, here.z_of(shift)),
                read_message(come_ref, stride * other, part),
            )
            for other in sides(part)
        ]

    write_messages(three_ref, part, through(down_ref, 2, -3))
    write_messages(one_ref, part, through(up_ref, 1, 1))


def arrivals(part, other, down_ref, *refs):
    return [read_message(down_ref, 2 * other + 1, part)] + [read_message(ref, other, part) for ref in refs]


def z_end(panel, rc_ref, *refs):
    here = Here(panel)
    *arrived, out_ref, sum_ref = refs
    value = base_value(SECOND, here, rc_ref, None, 1, here.z)
    write_messages(out_ref, SECOND, [lambda: add(value, *arrivals(SECOND, 1, *arrived))])
    mine = base_value(SECOND, here, rc_ref, None, 0, here.z)
    sum_ref[...] = add(mine, *arrivals(SECOND, 0, *arrived))[0]


def z_most(panel, rc_ref, rx_ref, down_ref, two_ref, far_ref, sum_ref):
    here = Here(panel)
    total = add(
        base_value(FIRST, here, rc_ref, rx_ref, 0, here.z),
        read_message(down_ref, 1, FIRST), read_message(two_ref, 0, FIRST), read_message(far_ref, 0, FIRST),
    )
    for i, block in enumerate(total):
        sum_ref[i * FIRST[1] : (i + 1) * FIRST[1], :] = block


def layer(most_ref, sum_ref, rx2_ref, three_ref, one_ref, weight_ref, out_ref):
    first = [most_ref[i * FIRST[1] : (i + 1) * FIRST[1], :] for i in range(FIRST[2])]
    first = add(first, read_message(three_ref, 0, FIRST), read_message(one_ref, 0, FIRST))
    second = add([sum_ref[...]], read_message(rx2_ref, 0, SECOND))
    weight = weight_ref[...]
    row = 0
    for block in first + second:
        high = block.astype(jnp.bfloat16)
        rest = block - high.astype(jnp.float32)
        middle = rest.astype(jnp.bfloat16)
        low = (rest - middle.astype(jnp.float32)).astype(jnp.bfloat16)
        result = jnp.dot(low, weight, preferred_element_type=jnp.float32)
        result += jnp.dot(middle, weight, preferred_element_type=jnp.float32)
        result += jnp.dot(high, weight, preferred_element_type=jnp.float32)
        out_ref[row : row + block.shape[0], :] = jnp.maximum(result, 0.0).astype(jnp.bfloat16)
        row += block.shape[0]


def send_blk(array, dy, flip=0):
    pairs = [(y * 2 + h, ((y + dy) % 4) * 2 + (h ^ flip)) for y in range(4) for h in range(2)]
    return lax.ppermute(array, "blk", pairs)


def send_rep(array, dx, dz, dc):
    pairs = [
        (x * 16 + z * 2 + c, (x ^ dx) * 16 + ((z + dz) % 8) * 2 + (c ^ dc))
        for x in range(2) for z in range(8) for c in range(2)
    ]
    return lax.ppermute(array, "rep", pairs)


def sum_along_z(part, name, panel, rc, rx):
    count = len(sides(part))
    have = (rc,) if rx is None else (rc, rx)

    def fill(kernel):
        if rx is not None:
            return functools.partial(kernel, part)
        return lambda panel_ref, rc_ref, *refs: kernel(part, panel_ref, rc_ref, None, *refs)

    down, up, two, far = call(
        fill(z_start), name + "_start", (messages(2 * count, part),) + (messages(count, part),) * 3,
        [VMEM] * (1 + len(have)), (VMEM,) * 4, (panel, *have), 0.6,
    )
    down, up = send_rep(down, 0, -1, 0), send_rep(up, 0, 1, 0)
    two, far = send_rep(two, 0, -2, 0), send_rep(far, 0, 3, 0)
    three, one = call(
        fill(z_middle), name + "_middle", (messages(count, part),) * 2,
        [VMEM] * (3 + len(have)), (VMEM,) * 2, (panel, *have, down, up), 0.6,
    )
    return down, two, far, send_rep(three, 0, -3, 0), send_rep(one, 0, 1, 0)


def local(node_feats, block_vals, block_rows, block_cols, block_count, weight):
    vals = block_vals.reshape(LISTS * SLOTS, BS, BS)
    panel_type = jax.ShapeDtypeStruct(((PANEL_BLK + 1) * BS, F), jnp.float32)
    here, near, far = ((0, False), (0, True)), ((3, False), (1, False), (3, True), (1, True), (2, False)), ((2, True),)
    own = node_feats
    flipped, below, above = send_blk(own, 0, 1), send_blk(own, 1), send_blk(own, -1)
    own = call(hold, "own_piece", jax.ShapeDtypeStruct((PIECE_ROWS, F), jnp.bfloat16), [VMEM], VMEM, (own,), 1)
    slots = block_rows.reshape(LISTS, SLOTS) * 4 + block_cols.reshape(LISTS, SLOTS)
    lists = slots * 64 + block_count.reshape(LISTS, 1)
    flipped, own, lists = lax.optimization_barrier((flipped, own, lists))
    below_flipped, above_flipped, far_own = send_blk(flipped, 1), send_blk(flipped, -1), send_blk(below, 1)
    later = len(near) + len(far)
    panel, next_vals = call(
        functools.partial(first_products, here, near + far), "products_here",
        (panel_type, jax.ShapeDtypeStruct((later * SLOTS, BS, BS), jnp.bfloat16)),
        [SMEM, VMEM, VMEM, ANY], (VMEM,) * 2, (lists, own, flipped, vals), 4, 40,
        scratch_shapes=[
            pltpu.VMEM((len(here), PIECE_ROWS, F), jnp.bfloat16),
            pltpu.VMEM((2 * SLOTS, BS, BS), jnp.bfloat16),
            pltpu.SemaphoreType.DMA((2 * GROUPS,)),
            pltpu.SemaphoreType.DMA((later * GROUPS,)),
        ],
    )
    panel, above, below_flipped, above_flipped, far_own = lax.optimization_barrier(
        (panel, above, below_flipped, above_flipped, far_own)
    )
    far_flipped = send_blk(above_flipped, -1)
    panel = call(
        functools.partial(more_products, near), "products_near", panel_type,
        [SMEM] + [VMEM] * 7, VMEM,
        (lists, panel, next_vals, below, above, below_flipped, above_flipped, far_own), 3, 24,
        input_output_aliases={1: 0},
        scratch_shapes=[pltpu.VMEM((len(near), PIECE_ROWS, F), jnp.bfloat16)],
    )
    panel, to_core = call(
        functools.partial(last_products, far[0], len(near)), "products_far", (panel_type, messages(8, FIRST)),
        [SMEM] + [VMEM] * 3, (VMEM,) * 2, (lists, panel, next_vals, far_flipped), 3, 24,
        input_output_aliases={1: 0},
    )

    rc_cross = send_rep(to_core, 0, 0, 1)
    second_rows, first_rows = messages(16, SECOND).shape[0], messages(8, FIRST).shape[0]
    to_core = call(
        rest_to_core, "core_rest", jax.ShapeDtypeStruct((second_rows + first_rows, F), jnp.int16),
        [VMEM], VMEM, (panel,), 0.3,
    )
    rc = send_rep(to_core, 0, 0, 1)
    to_x = call(x_messages, "x_first", messages(8, FIRST), [VMEM, VMEM], VMEM, (panel, rc_cross), 0.6)
    rx_first = send_rep(to_x, 1, 0, 0)
    second = sum_along_z(SECOND, "second", panel, rc, None)
    to_x, own_sum = call(
        z_end, "x_second", (messages(1, SECOND), jax.ShapeDtypeStruct((SECOND[1], F), jnp.float32)),
        [VMEM] * 7, (VMEM,) * 2, (panel, rc, *second), 0.6,
    )
    panel, to_x = lax.optimization_barrier((panel, to_x))
    rx_second = send_rep(to_x, 1, 0, 0)
    first = sum_along_z(FIRST, "first", panel, rc, rx_first)
    down, two, far, three, one = first
    most = call(
        z_most, "first_most", jax.ShapeDtypeStruct((FIRST[1] * FIRST[2], F), jnp.float32), [VMEM] * 6, VMEM,
        (panel, rc, rx_first, down, two, far), 0.3,
    )
    return call(
        layer, "layer", jax.ShapeDtypeStruct((PIECE_ROWS, H), jnp.bfloat16), [VMEM] * 6, VMEM,
        (most, own_sum, rx_second, three, one, weight), 1.0,
    )


def solution(mesh):
    return jax.shard_map(
        local,
        mesh=mesh,
        in_specs=(
            P(("blk", "rep"), None),
            P("blk", "rep", None, None, None, None),
            P("blk", "rep", None, None),
            P("blk", "rep", None, None),
            P("blk", "rep", None),
            P(),
        ),
        out_specs=P(("blk", "rep"), None),
        check_vma=False,
    )
```
